256 devices in a mesh: macro: 16 (over x, y), tile: 8 (over z), micro: 2 (over core).
Axes of the slice: x: 4, y: 4, z: 8, core: 2. Of those that a mesh axis runs over, the one named last changes fastest.
Arguments:
- velocity: float32 [3, 384, 64, 256], P(None, 'macro', 'tile', 'micro'), may hold values from -6 to 6
- viscosity: float32 [384, 64, 256], P('macro', 'tile', 'micro'), may hold values from 0.3 to 3
- flag_cell: int32 [8192], P(('macro', 'tile', 'micro')), may hold values from 1153 to 23422, as said below
- flag_owner: int32 [8192, 1], P(('macro', 'tile', 'micro')), may hold values from 0 to 31; in each aligned block of 32 rows (0 to 31, 32 to 63, ...) at most 2 rows name the same one
- conformations: float32 [3, 16384, 512], P(None, ('macro', 'tile', 'micro')), may hold values from -3.2 to 3.2
- increments: bfloat16 [16, 3, 16384, 512], P(None, None, ('macro', 'tile', 'micro')), may hold values from -4 to 4
Outputs:
- velocity_next: float32 [3, 384, 64, 256], P(None, 'macro', 'tile', 'micro')
- conformations_next: float32 [3, 16384, 512], P(None, ('macro', 'tile', 'micro'))
- flag_stress: float32 [6, 8192], P(None, ('macro', 'tile', 'micro'))
The draws below stay inside these ranges and needn't reach their ends.
Inputs may be any that keep to these rules, and one draw needn't show every extreme that they name: `flag_cell`: on each device 32 distinct cells of its own block, none of them on a face of the block. `flag_owner`: among the 32 entries of one device at most 2 name the same owner, and some device has an owner named 2 times.
All inputs are finite; a program needn't handle non-finite values.
Results may differ from the reference program's by a relative error of at most 0.0003.
Values sent between devices are 32-bit elements; how exact they have to be, the bound alone decides.
A program may use at most 64 MiB of HBM per device.

```python
import math
import jax
import jax.numpy as jnp
import numpy as np
from jax import lax

CX = 24
CY = 8
CZ = 128
F_DEV = 32
DUMBBELLS = 512
SUBSTEPS = 16
OWNERS = 32
CAP = 2
SLOTS = 64
ENS = 16384
FLAGS = 8192
NX = 384
NY = 64
NZ = 256
N_TILE = 8
N_MICRO = 2


def draw_flag_cell(key, part):
    device_count = FLAGS // F_DEV
    inner_count = (CX - 2) * (CY - 2) * (CZ - 2)
    device_keys = jax.random.split(key, device_count)

    def one_device(device_key):
        chosen = jax.random.permutation(device_key, inner_count)[:F_DEV].astype(jnp.int32)
        inner_x = chosen // ((CY - 2) * (CZ - 2)) + 1
        inner_y = chosen // (CZ - 2) % (CY - 2) + 1
        inner_z = chosen % (CZ - 2) + 1
        return ((inner_x * CY + inner_y) * CZ + inner_z).astype(jnp.int32)
    return jax.vmap(one_device)(device_keys).reshape(FLAGS)


def block_levels(own_key, dims, shards, smallest, largest):
    gain, own = 1.0, jax.random.fold_in(own_key, 6)
    for dim, blocks in shards:
        heights = jnp.exp(jax.random.uniform(jax.random.fold_in(own, dim), (blocks,), jnp.float32, smallest / len(shards), largest / len(shards)))
        gain = gain * jnp.repeat(heights, dims[dim] // blocks).reshape([-1 if axis == dim else 1 for axis in range(len(dims))])
    return gain


def assign_block(own_key, own, number, rows, count, top, reach, skew):
    ranking = jax.random.permutation(own_key, count)
    crowded, common = load_shares(count, rows * top, reach, skew, True), load_shares(count, rows * top, reach, skew, False)
    places = jnp.arange(count)

    def named(lengths, rotation):
        used = int((lengths > 0).sum())
        fixed = max(1, used // 4)
        shifted = fixed + (places - fixed + rotation * (used - fixed)) % max(1, count - fixed)
        return jnp.zeros((count,), jnp.int32).at[ranking[jnp.where(places < fixed, places, shifted)]].set(jnp.asarray(lengths, jnp.int32))

    lengths = jnp.where(number % 4 == 0, named(crowded, number // 4), named(common, number - number // 4 - 1))
    mixed = jax.random.permutation(jax.random.fold_in(own, 3), count)
    source_of, taker = mixed[0:count // 2 * 2:2], mixed[1:count // 2 * 2:2]
    slack = jnp.minimum(lengths[source_of] - 1, reach - lengths[taker]) // 2
    slack = jnp.where((source_of == ranking[0]) | (taker == ranking[0]) | (lengths[taker] == 0), 0, jnp.maximum(slack, 0))
    shifted = jax.random.randint(jax.random.fold_in(own, 4), (count // 2,), 0, 1 << 20) % (slack + 1)
    lengths = lengths.at[source_of].add(-shifted).at[taker].add(shifted)
    labels = jnp.searchsorted(jnp.cumsum(lengths), jnp.arange(rows * top), side="right").astype(jnp.int32)
    listing = labels.reshape(top, rows).T
    listing = listing[jax.random.permutation(jax.random.fold_in(own, 1), rows)]
    rotation = jax.random.randint(jax.random.fold_in(own, 2), (rows, 1), 0, top)
    return jnp.take_along_axis(listing, (jnp.arange(top)[None, :] + rotation) % top, axis=1)


def load_shares(amount, total, limit, slope, full):
    loads = [(1 << 20) // math.isqrt(rank ** slope) + 1 for rank in range(1, amount + 1)]
    largest = limit if full else min(limit, max(-(-total // amount), total * loads[0] // sum(loads)))
    least = 1 if total - largest >= amount - 1 else 0
    given, rest = [largest] + [least] * (amount - 1), total - largest - least * (amount - 1)
    while rest > 0:
        candidates = [i for i in range(1, amount) if given[i] < largest] or [i for i in range(1, amount) if given[i] < limit]
        mass, left = sum([loads[i] for i in candidates]), rest
        for i in candidates:
            addition = min(limit - given[i], max(1, left * loads[i] // mass), rest)
            given[i] = given[i] + addition
            rest = rest - addition
    return np.array(given)


def normal_values(rng, shape, spread, reach, shards=(), kind=jnp.bfloat16):
    factor_of = block_levels(rng, shape, shards, -0.22, 0.18) if shards else 1.0
    array = jax.random.normal(rng, shape, jnp.float32) * spread * factor_of
    return jnp.minimum(jnp.maximum(array, -reach), reach).astype(kind)


def setup_inputs(seed: int = 0) -> dict:
    arg_keys = jax.random.split(jax.random.key(seed), 7)
    velocity = normal_values(arg_keys[0], (3, NX, NY, NZ), 1.0, 6.0, ((1, 16), (2, 8), (3, 2)), jnp.float32)
    viscosity = jnp.clip(jnp.exp(math.log(3.0) - 2.3025851 * jax.random.uniform(arg_keys[1], (NX, NY, NZ), jnp.float32) ** block_levels(arg_keys[1], (NX, NY, NZ), ((0, 16), (1, 8), (2, 2)), -0.2, 0.2)), 0.3, 3.0)
    flag_cell = draw_flag_cell(jax.random.fold_in(arg_keys[6], 71), 0)
    flag_owner_keys = jax.random.split(jax.random.fold_in(arg_keys[3], 1), FLAGS // F_DEV)
    flag_owner_turns = jax.random.permutation(jax.random.fold_in(arg_keys[3], 3), FLAGS // F_DEV)
    flag_owner = jax.vmap(lambda own, number: assign_block(jax.random.fold_in(arg_keys[3], 2), own, number, F_DEV, OWNERS, 1, CAP, 2))(flag_owner_keys, flag_owner_turns).reshape((FLAGS, 1))
    conformations = jnp.clip(jax.random.uniform(arg_keys[4], (3, ENS, DUMBBELLS), jnp.float32, -3.2, 3.2) * block_levels(arg_keys[4], (3, ENS, DUMBBELLS), ((1, 256),), -0.4, 0.0), -3.2, 3.2)
    increments = normal_values(arg_keys[5], (SUBSTEPS, 3, ENS, DUMBBELLS), 1.0, 4.0, ((2, 256),))
    return {"velocity": velocity, "viscosity": viscosity, "flag_cell": flag_cell, "flag_owner": flag_owner, "conformations": conformations, "increments": increments}


stress_pairs = ((0, 0), (1, 1), (2, 2), (0, 1), (0, 2), (1, 2))
macro_step = 0.1
micro_step = 0.01
noise_weight = 0.1
relax_rate = 0.5
fene_extent = 30.0
spring_floor = 0.1
polymer_weight = 0.25


def pair_index(left_axis, right_axis):
    return stress_pairs.index((min(left_axis, right_axis), max(left_axis, right_axis)))


def window(source, direction, offset):
    slicers = [slice(None)]
    for spatial in range(3):
        length = source.shape[spatial + 1] - 2
        if spatial == direction:
            slicers.append(slice(offset, offset + length))
        else:
            slicers.append(slice(1, 1 + length))
    return source[tuple(slicers)]


def stress_field(padded, viscous):
    slopes = [(window(padded, direction, 2) - window(padded, direction, 0)) * 0.5 for direction in range(3)]
    components = [viscous * (slopes[right_axis][left_axis] + slopes[left_axis][right_axis]) for left_axis, right_axis in stress_pairs]
    return jnp.stack(components, axis=0)


def divergence(padded_stress):
    result = []
    for left_axis in range(3):
        summed = None
        for right_axis in range(3):
            member = pair_index(left_axis, right_axis)
            column = padded_stress[member:member + 1]
            change = (window(column, right_axis, 2) - window(column, right_axis, 0))[0] * 0.5
            summed = change if summed is None else summed + change
        result.append(summed)
    return jnp.stack(result, axis=0)


def spring_of(current):
    return 1.0 / jnp.maximum(1.0 - (current[0] * current[0] + current[1] * current[1] + current[2] * current[2]) / fene_extent, spring_floor)


def advance(conform, gradient_in, noise):
    rate_table = gradient_in[:, :, None]

    def substep(substep_index, current):
        spring = spring_of(current)
        updated = []
        for left_axis in range(3):
            drift_term = rate_table[3 * left_axis] * current[0] + rate_table[3 * left_axis + 1] * current[1] + rate_table[3 * left_axis + 2] * current[2] - relax_rate * spring * current[left_axis]
            updated.append(current[left_axis] + micro_step * drift_term + noise_weight * noise[substep_index, left_axis].astype(jnp.float32))
        return jnp.stack(updated, axis=0)

    last_state = lax.fori_loop(0, noise.shape[0], substep, conform)
    spring = spring_of(last_state)
    stresses = []
    for left_axis, right_axis in stress_pairs:
        identity_part = 1.0 if left_axis == right_axis else 0.0
        stresses.append(polymer_weight * (jnp.mean(spring * last_state[left_axis] * last_state[right_axis], axis=-1) - identity_part))
    return last_state, jnp.stack(stresses, axis=0)


def reference(velocity, viscosity, flag_cell, flag_owner, conformations, increments):
    device_count = FLAGS // F_DEV
    device_of = jnp.arange(FLAGS, dtype=jnp.int32) // F_DEV
    macro_of = device_of // (N_TILE * N_MICRO)
    tile_of = (device_of // N_MICRO) % N_TILE
    micro_of = device_of % N_MICRO
    local_x = flag_cell // (CY * CZ)
    local_y = (flag_cell // CZ) % CY
    local_z = flag_cell % CZ
    global_x = macro_of * CX + local_x
    global_y = tile_of * CY + local_y
    global_z = micro_of * CZ + local_z
    slopes = []
    for shift_x, shift_y, shift_z in ((1, 0, 0), (0, 1, 0), (0, 0, 1)):
        upper_side = velocity[:, global_x + shift_x, global_y + shift_y, global_z + shift_z]
        lower_side = velocity[:, global_x - shift_x, global_y - shift_y, global_z - shift_z]
        slopes.append((upper_side - lower_side) * 0.5)
    gradient_rows = jnp.stack(slopes, axis=1).reshape(9, FLAGS)
    owner_index = flag_owner[:, 0]
    onehot = (owner_index[:, None] == jnp.arange(OWNERS, dtype=jnp.int32)[None, :]).astype(jnp.int32)
    onehot = onehot.reshape(device_count, F_DEV, OWNERS)
    earlier = jnp.cumsum(onehot, axis=1) - onehot
    slot_rank = jnp.sum(earlier * onehot, axis=2).reshape(FLAGS)
    sender = macro_of * N_MICRO + micro_of
    owner_device = ((owner_index // N_MICRO) * N_TILE + tile_of) * N_MICRO + owner_index % N_MICRO
    target = (owner_device * SLOTS + sender * CAP + slot_rank).astype(jnp.int32)
    gradient_in = jnp.zeros((9, ENS), jnp.float32).at[:, target].set(gradient_rows)
    last_state, polymer = advance(conformations, gradient_in, increments)
    polymer_rows = polymer[:, target]
    padded = jnp.pad(velocity, ((0, 0), (1, 1), (1, 1), (1, 1)))
    stress_all = stress_field(padded, viscosity)
    stress_all = stress_all.at[:, global_x, global_y, global_z].add(polymer_rows)
    flag_stress = stress_all[:, global_x, global_y, global_z]
    stress_pad = jnp.pad(stress_all, ((0, 0), (1, 1), (1, 1), (1, 1)))
    velocity_next = velocity + macro_step * divergence(stress_pad)
    return (velocity_next, last_state, flag_stress)
```

```python
import functools
import math

import jax
import jax.numpy as jnp
from jax import lax
from jax.experimental import pallas as pl
from jax.experimental.pallas import tpu as pltpu
from jax.sharding import PartitionSpec as P

MESH = pl.DeviceIdType.MESH
F32, BF16, I32 = jnp.float32, jnp.bfloat16, jnp.int32

PAIRS = ((0, 0), (1, 1), (2, 2), (0, 1), (0, 2), (1, 2))
SIDE = ((0, 3, 4), (3, 1, 5), (4, 5, 2))
SCALE = math.sqrt(200.0 / 30.0)

NX, NY, NZ = 24, 8, 128
ROWS = NX * NY
FLAG = 32
SLOTS = 64
BEADS = 512
STEPS = 16
BLOCK = 16
GROUP = BLOCK // 2
NBLOCK = SLOTS // BLOCK


def iota(shape, dim):
    return lax.broadcasted_iota(I32, shape, dim)


def pieces(x, count):
    out = []
    for _ in range(count):
        part = x.astype(BF16)
        out.append(part)
        x = x - part.astype(F32)
    return out


def dot(a, b):
    return jnp.dot(a, b, preferred_element_type=F32)


def kernel(
    n_macro, n_tile, n_micro,
    v_in, visc_in, cell_s_in, cell_in, owner_s_in, owner_in, conf_in, noise_in,
    vel_out, conf_out, fs_out,
    vp, visc, cells, cellv, owners, ownerv, rankv, ranks, q, nz, nf, gat, grow, vrow, prow,
    kst, kb, pol, send1, recv1, send2, recv2,
    yp1, zp1, hx1, hy1, hz1, sp, xp2, yp2, zp2, hx2, hy2, hz2, amat, vel,
    in_sem, out_sem, s1_sem, r1_sem, s2_sem, r2_sem, hs1_sem, hr1_sem, hs2_sem, hr2_sem,
):
    macro, tile, micro = lax.axis_index("macro"), lax.axis_index("tile"), lax.axis_index("micro")
    owners_n = n_macro * n_micro
    me = macro * n_micro + micro
    my_block = lax.div(me, GROUP)

    loads = [
        pltpu.make_async_copy(v_in, vp.at[:, pl.ds(NY, ROWS), :], in_sem.at[0]),
        pltpu.make_async_copy(cell_s_in, cells, in_sem.at[1]),
        pltpu.make_async_copy(cell_in, cellv, in_sem.at[2]),
        pltpu.make_async_copy(owner_s_in, owners, in_sem.at[3]),
        pltpu.make_async_copy(owner_in, ownerv, in_sem.at[4]),
        pltpu.make_async_copy(visc_in, visc, in_sem.at[5]),
        pltpu.make_async_copy(noise_in, nz, in_sem.at[6]),
        pltpu.make_async_copy(conf_in, q, in_sem.at[7]),
    ]
    for load in loads:
        load.start()

    barrier = pltpu.get_barrier_semaphore()

    def greet(k, carry):
        peer = lax.rem(me + k, owners_n)
        pl.semaphore_signal(
            barrier, inc=1,
            device_id=(lax.div(peer, n_micro), tile, lax.rem(peer, n_micro)), device_id_type=MESH,
        )
        return carry

    lax.fori_loop(1, owners_n, greet, 0)
    tile_up, tile_down = lax.rem(tile + 1, n_tile), lax.rem(tile + n_tile - 1, n_tile)
    macro_up, macro_down = lax.rem(macro + 1, n_macro), lax.rem(macro + n_macro - 1, n_macro)
    for target in (tile_up, tile_down):
        pl.semaphore_signal(barrier, inc=1, device_id=(macro, target, micro), device_id_type=MESH)

    for load in loads[:6]:
        load.wait()

    def gather(j, carry):
        row = lax.shift_right_logical(cells[j], 7) + NY
        for a in range(3):
            read = lambda offset: vp[a, pl.ds(row + offset, 1), :]
            gat[3 * a, pl.ds(j, 1), :] = read(NY) - read(-NY)
            gat[3 * a + 1, pl.ds(j, 1), :] = read(1) - read(-1)
            gat[3 * a + 2, pl.ds(j, 1), :] = read(0)
        gat[9, pl.ds(j, 1), :] = visc[pl.ds(row - NY, 1), :]
        return carry

    lax.fori_loop(0, FLAG, gather, 0, unroll=8)

    square0, square1 = iota((FLAG, FLAG), 0), iota((FLAG, FLAG), 1)

    def column(row):
        return jnp.sum(jnp.where(square0 == square1, row, 0), axis=1, keepdims=True)

    cell_row, owner_row = cellv[...], ownerv[...]
    cell_col, owner_col = column(cell_row), column(owner_row)
    z_col = cell_col & (NZ - 1)
    lane = iota((FLAG, NZ), 1)
    here, above, below = lane == z_col, lane == z_col + 1, lane == z_col - 1
    rank_row = jnp.sum(
        jnp.where((square0 < square1) & (owner_col == owner_row), 1, 0), axis=0, keepdims=True
    )
    rankv[...] = jnp.minimum(rank_row, 1)
    rank_copy = pltpu.make_async_copy(rankv, ranks, in_sem.at[8])
    rank_copy.start()

    gathered = jnp.zeros((FLAG, NZ), F32)
    columns = []
    for k in range(10):
        values = gat[k]
        if k < 9 and k % 3 == 2:
            picked = jnp.where(above, values, 0.0) - jnp.where(below, values, 0.0)
        else:
            picked = jnp.where(here, values, 0.0)
        if k < 9:
            picked = picked * 0.5
        columns.append(jnp.sum(picked, axis=1, keepdims=True))
        gathered = jnp.where(lane == k, columns[k], gathered)
    position = owner_row * 2 + rank_row
    placing = (iota((SLOTS, FLAG), 0) == position).astype(F32).astype(BF16)
    hi, mid, lo = pieces(gathered, 3)
    outgoing = dot(placing, hi) + (dot(placing, mid) + dot(placing, lo))
    for s in range(owners_n):
        send1[s] = outgoing[2 * s : 2 * s + 2, :]

    pl.semaphore_wait(barrier, owners_n + 1)

    def peer_id(peer):
        return (lax.div(peer, n_micro), tile, lax.rem(peer, n_micro))

    def block_of(order, sign):
        shift = (0, 1, NBLOCK - 1, 2)[order]
        return lax.rem(my_block + sign * shift + NBLOCK, NBLOCK)

    def post(block, send, recv, send_sem, recv_sem):
        def one(k, carry):
            peer = block * GROUP + lax.rem(me + k, GROUP)

            @pl.when(peer != me)
            def _():
                pltpu.make_async_remote_copy(
                    src_ref=send.at[peer], dst_ref=recv.at[me],
                    send_sem=send_sem, recv_sem=recv_sem.at[my_block],
                    device_id=peer_id(peer), device_id_type=MESH,
                ).start()

            @pl.when(peer == me)
            def _():
                pltpu.make_async_copy(send.at[me], recv.at[me], recv_sem.at[my_block]).start()

            return carry

        lax.fori_loop(0, GROUP, one, 0)

    def arrive(block, recv, recv_sem):
        part = recv.at[pl.ds(block * GROUP, GROUP)]
        pltpu.make_async_copy(part, part, recv_sem.at[block]).wait()

    def sent(send, send_sem):
        part = send.at[pl.ds(0, owners_n - 1)]
        pltpu.make_async_copy(part, part, send_sem).wait()

    for order in range(NBLOCK):
        post(block_of(order, -1), send1, recv1, s1_sem, r1_sem)

    sub, lanes = iota((NY, NZ), 0), iota((NY, NZ), 1)
    face = jnp.where(micro == 0, NZ - 1, 0)

    def pack_z(read):
        def one(x, carry):
            return tuple(
                total + pltpu.roll(jnp.where(lanes == face, value, 0.0), x, 1)
                for total, value in zip(carry, read(x))
            )

        return lax.fori_loop(0, NX, one, tuple(jnp.zeros((NY, NZ), F32) for _ in range(3)), unroll=4)

    for a in range(3):
        yp1[0, a] = vp[a, pl.ds(NY, NX, stride=NY), :]
        yp1[1, a] = vp[a, pl.ds(2 * NY - 1, NX, stride=NY), :]

    def rows_of(x):
        return pl.ds(pl.multiple_of((x + 1) * NY, NY), NY)

    packed = pack_z(lambda x: [vp[a, rows_of(x), :] for a in range(3)])
    for a in range(3):
        zp1[a] = packed[a]

    def halo_copies(x_low, x_high, y_pack, z_pack, hx, hy, hz, send_sem, recv_sem):
        def remote(i, src, dst, target):
            return pltpu.make_async_remote_copy(
                src_ref=src, dst_ref=dst, send_sem=send_sem.at[i], recv_sem=recv_sem.at[i],
                device_id=target, device_id_type=MESH,
            )

        return [
            remote(0, x_high, hx.at[0], (macro_up, tile, micro)),
            remote(1, x_low, hx.at[1], (macro_down, tile, micro)),
            remote(2, y_pack.at[1], hy.at[0], (macro, tile_up, micro)),
            remote(3, y_pack.at[0], hy.at[1], (macro, tile_down, micro)),
            remote(4, z_pack, hz, (macro, tile, 1 - micro)),
        ]

    halo1 = halo_copies(
        vp.at[:, pl.ds(NY, NY), :], vp.at[:, pl.ds(ROWS, NY), :], yp1, zp1, hx1, hy1, hz1, hs1_sem, hr1_sem
    )
    for copy in halo1:
        copy.start()

    loads[6].wait()

    def widen(t, carry):
        for a in range(3):
            nf[t, a] = nz[t, a].astype(F32) * (0.1 * SCALE)
        return carry

    lax.fori_loop(0, STEPS, widen, 0)
    loads[7].wait()
    for a in range(3):
        q[a] = q[a] * SCALE

    def chunk(c):
        return pl.ds(c * 128, 128)

    def block_work(order, carry):
        shift = jnp.where(order == 0, 0, jnp.where(order == 1, 1, jnp.where(order == 2, NBLOCK - 1, 2)))
        block = lax.rem(my_block + shift, NBLOCK)
        arrive(block, recv1, r1_sem)
        slots = pl.ds(pl.multiple_of(block * BLOCK, BLOCK), BLOCK)
        for s in range(GROUP):
            kst[pl.ds(2 * s, 2), :] = recv1[block * GROUP + s]
        kappa = kst[...] * 0.01
        for k in range(9):
            wide = jnp.broadcast_to(kappa[:, k : k + 1], (BLOCK, 128))
            kb[k] = wide + 1.0 if k % 4 == 0 else wide

        def step(t, state):
            new = []
            for c in range(BEADS // 128):
                q0, q1, q2 = state[3 * c : 3 * c + 3]
                pull = pltpu.reciprocal(
                    jnp.maximum(200.0 - q0 * q0 - (q1 * q1 + q2 * q2), 20.0), approx=True
                )
                for a in range(3):
                    here_q = (q0, q1, q2)[a]
                    other = [b for b in range(3) if b != a]
                    new.append(
                        (kb[4 * a] - pull) * here_q
                        + (kb[3 * a + other[0]] * (q0, q1, q2)[other[0]] + kb[3 * a + other[1]] * (q0, q1, q2)[other[1]])
                        + nf[t, a, slots, chunk(c)]
                    )
            return tuple(new)

        state = tuple(q[a, slots, chunk(c)] for c in range(BEADS // 128) for a in range(3))
        state = lax.fori_loop(0, STEPS, step, state, unroll=2)
        sums = [None] * 6
        for c in range(BEADS // 128):
            values = state[3 * c : 3 * c + 3]
            q0, q1, q2 = values
            pull = 1.0 / jnp.maximum(200.0 - (q0 * q0 + q1 * q1 + q2 * q2), 20.0)
            for a in range(3):
                q[a, slots, chunk(c)] = values[a] * (1.0 / SCALE)
            for k, (a, b) in enumerate(PAIRS):
                term = pull * values[a] * values[b]
                sums[k] = term if sums[k] is None else sums[k] + term
        lane16 = iota((BLOCK, 128), 1)
        stresses = jnp.zeros((BLOCK, 128), F32)
        for k, (a, b) in enumerate(PAIRS):
            mean = jnp.sum(sums[k], axis=1, keepdims=True) * (30.0 / BEADS)
            stresses = jnp.where(lane16 == k, 0.25 * (mean - (1.0 if a == b else 0.0)), stresses)
        pol[...] = stresses
        for s in range(GROUP):
            send2[block * GROUP + s] = pol[pl.ds(2 * s, 2), :]
        post(block, send2, recv2, s2_sem, r2_sem)
        pltpu.make_async_copy(q.at[:, slots, :], conf_out.at[:, slots, :], out_sem.at[0]).start()
        return carry

    lax.fori_loop(0, NBLOCK, block_work, 0)

    for copy in halo1:
        copy.wait()

    def keep(condition):
        return jnp.where(condition, 1.0, 0.0)

    x_low, x_high = keep(macro > 0), keep(macro < n_macro - 1)
    y_low, y_high = keep(tile > 0), keep(tile < n_tile - 1)
    first_lane, last_lane = lanes == 0, lanes == NZ - 1
    z_high, z_low = keep(micro == 0), keep(micro == 1)

    def slope_y(value, hy, a, x):
        low = hy[0, a, pl.ds(x, 1), :] * y_low
        high = hy[1, a, pl.ds(x, 1), :] * y_high
        up = jnp.where(sub == NY - 1, high, pltpu.roll(value, NY - 1, 0))
        down = jnp.where(sub == 0, low, pltpu.roll(value, 1, 0))
        return up - down

    def slope_z(value, hz, a, x):
        beside = pltpu.roll(hz[a], lax.rem(NZ - x, NZ), 1)
        up = pltpu.roll(jnp.where(first_lane, beside * z_high, value), NZ - 1, 1)
        down = pltpu.roll(jnp.where(last_lane, beside * z_low, value), 1, 1)
        return up - down

    for a in range(3):
        vp[a, pl.ds(0, NY), :] = hx1[0, a] * x_low
        vp[a, pl.ds(ROWS + NY, NY), :] = hx1[1, a] * x_high

    def stress_at(x, carry):
        grad = {}
        for a in range(3):
            value = vp[a, rows_of(x), :]
            grad[a, 0] = vp[a, rows_of(x + 1), :] - vp[a, rows_of(x - 1), :]
            grad[a, 1] = slope_y(value, hy1, a, x)
            grad[a, 2] = slope_z(value, hz1, a, x)
        half = visc[pl.ds(pl.multiple_of(x * NY, NY), NY), :] * 0.5
        for k, (a, b) in enumerate(PAIRS):
            sp[k, rows_of(x), :] = half * (grad[a, b] + grad[b, a])
        return carry

    lax.fori_loop(0, NX, stress_at, 0, unroll=2)

    for a in range(3):
        xp2[0, a] = sp[SIDE[0][a], pl.ds(NY, NY), :]
        xp2[1, a] = sp[SIDE[0][a], pl.ds(ROWS, NY), :]
        yp2[0, a] = sp[SIDE[1][a], pl.ds(NY, NX, stride=NY), :]
        yp2[1, a] = sp[SIDE[1][a], pl.ds(2 * NY - 1, NX, stride=NY), :]
    packed = pack_z(lambda x: [sp[SIDE[2][a], rows_of(x), :] for a in range(3)])
    for a in range(3):
        zp2[a] = packed[a]
    halo2 = halo_copies(xp2.at[0], xp2.at[1], yp2, zp2, hx2, hy2, hz2, hs2_sem, hr2_sem)
    for copy in halo2:
        copy.start()

    viscous = jnp.zeros((FLAG, NZ), F32)
    for k, (a, b) in enumerate(PAIRS):
        viscous = jnp.where(lane == k, columns[9] * (columns[3 * a + b] + columns[3 * b + a]), viscous)
    vrow[...] = viscous
    row_col = lax.shift_right_logical(cell_col, 7)
    six = jnp.concatenate([row_col] * 6, axis=0)
    wide0, wide1 = iota((ROWS, ROWS), 0), iota((ROWS, ROWS), 1)
    six_row = jnp.sum(jnp.where(wide0 == wide1, six, 0), axis=0, keepdims=True)
    offset = jnp.where(wide1 < 64, NY, jnp.where(wide1 < 128, 1, 0))
    plus = jnp.where(wide0 == six_row - offset, 1.0, 0.0)
    minus = jnp.where((wide0 == six_row + offset) & (wide1 < 128), 1.0, 0.0)
    amat[...] = (plus - minus).astype(BF16)

    for copy in halo2:
        copy.wait()
    for a in range(3):
        sp[SIDE[0][a], pl.ds(0, NY), :] = hx2[0, a] * x_low
        sp[SIDE[0][a], pl.ds(ROWS + NY, NY), :] = hx2[1, a] * x_high

    def advance_at(x, carry):
        for a in range(3):
            total = sp[SIDE[0][a], rows_of(x + 1), :] - sp[SIDE[0][a], rows_of(x - 1), :]
            total = total + slope_y(sp[SIDE[1][a], rows_of(x), :], hy2, a, x)
            total = total + slope_z(sp[SIDE[2][a], rows_of(x), :], hz2, a, x)
            vel[a, pl.ds(pl.multiple_of(x * NY, NY), NY), :] = vp[a, rows_of(x), :] + 0.05 * total
        return carry

    lax.fori_loop(0, NX, advance_at, 0, unroll=2)

    rank_copy.wait()
    for block in range(NBLOCK):
        arrive(block, recv2, r2_sem)

    def collect(j, carry):
        prow[pl.ds(j, 1), :] = recv2[owners[j], pl.ds(ranks[0, j], 1), :]
        return carry

    lax.fori_loop(0, FLAG, collect, 0, unroll=8)
    returned = prow[...]
    flagged = vrow[...] + jnp.where(lane < 6, returned, 0.0)
    pick = (iota((8, NZ), 0) == iota((8, NZ), 1)).astype(F32).astype(BF16)
    turned = None
    for part in pieces(flagged, 3):
        term = lax.dot_general(pick, part, (((1,), (1,)), ((), ())), preferred_element_type=F32)
        turned = term if turned is None else turned + term
    fs_out[...] = turned[:6, :]

    spread = [jnp.broadcast_to(returned[:, k : k + 1] * 0.05, (FLAG, NZ)) for k in range(6)]
    for a in range(3):
        parts = []
        parts += pieces(jnp.where(here, spread[SIDE[0][a]], 0.0), 2)
        parts += pieces(jnp.where(here, spread[SIDE[1][a]], 0.0), 2)
        parts += pieces(
            jnp.where(below, spread[SIDE[2][a]], 0.0) - jnp.where(above, spread[SIDE[2][a]], 0.0), 2
        )
        vel[a] = vel[a] + dot(amat[...], jnp.concatenate(parts, axis=0))
        pltpu.make_async_copy(vel.at[a], vel_out.at[a], out_sem.at[1]).start()

    pltpu.make_async_copy(vel, vel_out, out_sem.at[1]).wait()
    pltpu.make_async_copy(q, conf_out, out_sem.at[0]).wait()
    sent(send1, s1_sem)
    sent(send2, s2_sem)


def shards(sizes, velocity, viscosity, flag_cell, flag_owner, conformations, increments):
    owner = flag_owner.reshape(FLAG)
    any_spec = pl.BlockSpec(memory_space=pltpu.HBM)
    vmem = lambda *shape: pltpu.VMEM(shape, F32)
    scratch = [
        vmem(3, ROWS + 2 * NY, NZ), vmem(ROWS, NZ),
        pltpu.SMEM((FLAG,), I32), pltpu.VMEM((1, FLAG), I32),
        pltpu.SMEM((FLAG,), I32), pltpu.VMEM((1, FLAG), I32),
        pltpu.VMEM((1, FLAG), I32), pltpu.SMEM((1, FLAG), I32),
        vmem(3, SLOTS, BEADS),
        pltpu.VMEM((STEPS, 3, SLOTS, BEADS), BF16), vmem(STEPS, 3, SLOTS, BEADS),
        vmem(10, FLAG, NZ), vmem(FLAG, NZ), vmem(FLAG, NZ), vmem(FLAG, NZ),
        vmem(BLOCK, 128), vmem(9, BLOCK, 128), vmem(BLOCK, 128),
        vmem(32, 2, 128), vmem(32, 2, 128), vmem(32, 2, 128), vmem(32, 2, 128),
        vmem(2, 3, NX, NZ), vmem(3, NY, NZ), vmem(2, 3, NY, NZ), vmem(2, 3, NX, NZ), vmem(3, NY, NZ),
        vmem(6, ROWS + 2 * NY, NZ),
        vmem(2, 3, NY, NZ), vmem(2, 3, NX, NZ), vmem(3, NY, NZ),
        vmem(2, 3, NY, NZ), vmem(2, 3, NX, NZ), vmem(3, NY, NZ),
        pltpu.VMEM((ROWS, ROWS), BF16), vmem(3, ROWS, NZ),
        pltpu.SemaphoreType.DMA((9,)), pltpu.SemaphoreType.DMA((2,)),
        pltpu.SemaphoreType.DMA, pltpu.SemaphoreType.DMA((NBLOCK,)),
        pltpu.SemaphoreType.DMA, pltpu.SemaphoreType.DMA((NBLOCK,)),
        pltpu.SemaphoreType.DMA((5,)), pltpu.SemaphoreType.DMA((5,)),
        pltpu.SemaphoreType.DMA((5,)), pltpu.SemaphoreType.DMA((5,)),
    ]
    vel, conf, stress = pl.pallas_call(
        functools.partial(kernel, *sizes),
        out_shape=(
            jax.ShapeDtypeStruct((3, ROWS, NZ), F32),
            jax.ShapeDtypeStruct(conformations.shape, F32),
            jax.ShapeDtypeStruct((6, FLAG), F32),
        ),
        in_specs=[any_spec] * 8,
        out_specs=(any_spec, any_spec, pl.BlockSpec(memory_space=pltpu.VMEM)),
        scratch_shapes=scratch,
        compiler_params=pltpu.CompilerParams(
            collective_id=0, has_side_effects=True, vmem_limit_bytes=56 * 2**20
        ),
    )(
        velocity.reshape(3, ROWS, NZ), viscosity.reshape(ROWS, NZ),
        flag_cell, flag_cell.reshape(1, FLAG), owner, owner.reshape(1, FLAG),
        conformations, increments,
    )
    return vel.reshape(velocity.shape), conf, stress


def solution(mesh):
    sizes = (mesh.shape["macro"], mesh.shape["tile"], mesh.shape["micro"])
    in_specs = (
        P(None, "macro", "tile", "micro"),
        P("macro", "tile", "micro"),
        P(("macro", "tile", "micro")),
        P(("macro", "tile", "micro"), None),
        P(None, ("macro", "tile", "micro"), None),
        P(None, None, ("macro", "tile", "micro"), None),
    )
    out_specs = (
        P(None, "macro", "tile", "micro"),
        P(None, ("macro", "tile", "micro"), None),
        P(None, ("macro", "tile", "micro")),
    )
    return jax.shard_map(
        functools.partial(shards, sizes), mesh=mesh, in_specs=in_specs, out_specs=out_specs, check_vma=False
    )
```

```python
import functools
import math

import jax
import jax.numpy as jnp
from jax import lax
from jax.experimental import pallas as pl
from jax.experimental.pallas import tpu as pltpu
from jax.sharding import PartitionSpec as P

MESH = pl.DeviceIdType.MESH
F32, BF16, I32 = jnp.float32, jnp.bfloat16, jnp.int32

PAIRS = ((0, 0), (1, 1), (2, 2), (0, 1), (0, 2), (1, 2))
SIDE = ((0, 3, 4), (3, 1, 5), (4, 5, 2))
SCALE = math.sqrt(200.0 / 30.0)

NX, NY, NZ = 24, 8, 128
ROWS = NX * NY
FLAG = 32
SLOTS = 64
BEADS = 512
STEPS = 16
BLOCK = 16
GROUP = BLOCK // 2
NBLOCK = SLOTS // BLOCK
STRESS_AT = 2
UNROLL = 4


def iota(shape, dim):
    return lax.broadcasted_iota(I32, shape, dim)


def pieces(x, count):
    out = []
    for _ in range(count):
        part = x.astype(BF16)
        out.append(part)
        x = x - part.astype(F32)
    return out


def dot(a, b):
    return jnp.dot(a, b, preferred_element_type=F32)


def kernel(
    n_macro, n_tile, n_micro,
    v, visc, cells_in, cellv, owners_in, ownerv, conf, noise_in,
    vel_out, conf_out, fs_out,
    cells, owners, rankv, ranks, q, nz, nf, gat, vrow, prow,
    kst, kb, pol, send1, recv1, send2, recv2,
    yp1, zp1, hx1, hy1, hz1, sp, xp2, yp2, zp2, hx2, hy2, hz2, amat,
    in_sem, s1_sem, r1_sem, s2_sem, r2_sem, hs1_sem, hr1_sem, hs2_sem, hr2_sem,
):
    macro, tile, micro = lax.axis_index("macro"), lax.axis_index("tile"), lax.axis_index("micro")
    owners_n = n_macro * n_micro
    me = macro * n_micro + micro
    my_block = lax.div(me, GROUP)

    loads = [
        pltpu.make_async_copy(cells_in, cells, in_sem.at[0]),
        pltpu.make_async_copy(owners_in, owners, in_sem.at[1]),
        pltpu.make_async_copy(noise_in, nz, in_sem.at[2]),
    ]
    for load in loads:
        load.start()

    barrier = pltpu.get_barrier_semaphore()
    has_up, has_down = tile < n_tile - 1, tile > 0

    def peer_id(peer):
        return (lax.div(peer, n_micro), tile, lax.rem(peer, n_micro))

    def greet(k, carry):
        pl.semaphore_signal(
            barrier, inc=1, device_id=peer_id(lax.rem(me + k, owners_n)), device_id_type=MESH
        )
        return carry

    lax.fori_loop(1, owners_n, greet, 0, unroll=True)

    @pl.when(has_up)
    def _():
        pl.semaphore_signal(barrier, inc=1, device_id=(macro, tile + 1, micro), device_id_type=MESH)

    @pl.when(has_down)
    def _():
        pl.semaphore_signal(barrier, inc=1, device_id=(macro, tile - 1, micro), device_id_type=MESH)

    loads[0].wait()

    def gather(j, carry):
        row = lax.shift_right_logical(cells[j], 7)
        row = jnp.minimum(jnp.maximum(row, NY), ROWS - NY - 1)
        for a in range(3):
            read = lambda offset: v[a, pl.ds(row + offset, 1), :]
            gat[3 * a, pl.ds(j, 1), :] = read(NY) - read(-NY)
            gat[3 * a + 1, pl.ds(j, 1), :] = read(1) - read(-1)
            gat[3 * a + 2, pl.ds(j, 1), :] = read(0)
        gat[9, pl.ds(j, 1), :] = visc[pl.ds(row, 1), :]
        return carry

    lax.fori_loop(0, FLAG, gather, 0, unroll=8)

    square0, square1 = iota((FLAG, FLAG), 0), iota((FLAG, FLAG), 1)

    def column(row):
        return jnp.sum(jnp.where(square0 == square1, row, 0), axis=1, keepdims=True)

    cell_row, owner_row = cellv[...], ownerv[...]
    cell_col, owner_col = column(cell_row), column(owner_row)
    z_col = cell_col & (NZ - 1)
    lane = iota((FLAG, NZ), 1)
    here, above, below = lane == z_col, lane == z_col + 1, lane == z_col - 1
    rank_row = jnp.sum(
        jnp.where((square0 < square1) & (owner_col == owner_row), 1, 0), axis=0, keepdims=True
    )
    rankv[...] = jnp.minimum(rank_row, 1)
    rank_copy = pltpu.make_async_copy(rankv, ranks, in_sem.at[3])
    rank_copy.start()

    gathered = jnp.zeros((FLAG, NZ), F32)
    columns = []
    for k in range(10):
        values = gat[k]
        if k < 9 and k % 3 == 2:
            picked = jnp.where(above, values, 0.0) - jnp.where(below, values, 0.0)
        else:
            picked = jnp.where(here, values, 0.0)
        if k < 9:
            picked = picked * 0.5
        columns.append(jnp.sum(picked, axis=1, keepdims=True))
        if k < 9:
            gathered = jnp.where(lane == k, columns[k], gathered)
    position = owner_row * 2 + rank_row
    placing = (iota((SLOTS, FLAG), 0) == position).astype(F32).astype(BF16)
    hi, mid, lo = pieces(gathered, 3)
    outgoing = dot(placing, hi) + (dot(placing, mid) + dot(placing, lo))
    for s in range(owners_n):
        send1[s] = outgoing[2 * s : 2 * s + 2, :]

    @pl.when(has_up & has_down)
    def _():
        pl.semaphore_wait(barrier, owners_n + 1)

    @pl.when(jnp.logical_not(has_up & has_down))
    def _():
        pl.semaphore_wait(barrier, owners_n)

    def block_of(order, sign):
        shift = (0, 1, NBLOCK - 1, 2)[order]
        return lax.rem(my_block + sign * shift + NBLOCK, NBLOCK)

    def post(order, block, send, recv, send_sem, recv_sem):
        if order == 0:
            recv[me] = send[me]
        base = block * GROUP
        turn = me - my_block * GROUP
        for k in range(1 if order == 0 else 0, GROUP):
            peer = base + lax.rem(turn + k, GROUP)
            pltpu.make_async_remote_copy(
                src_ref=send.at[peer], dst_ref=recv.at[me],
                send_sem=send_sem, recv_sem=recv_sem.at[my_block],
                device_id=peer_id(peer), device_id_type=MESH,
            ).start()

    def arrive(order, block, recv, recv_sem):
        part = recv.at[pl.ds(0, GROUP - 1 if order == 0 else GROUP)]
        pltpu.make_async_copy(part, part, recv_sem.at[block]).wait()

    def sent(send, send_sem):
        part = send.at[pl.ds(0, owners_n - 1)]
        pltpu.make_async_copy(part, part, send_sem).wait()

    for order in range(NBLOCK):
        post(order, block_of(order, -1), send1, recv1, s1_sem, r1_sem)

    sub, lanes = iota((NY, NZ), 0), iota((NY, NZ), 1)
    face = lanes == jnp.where(micro == 0, NZ - 1, 0)
    first_lane, last_lane = lanes == 0, lanes == NZ - 1
    first_row, last_row = sub == 0, sub == NY - 1

    def rows_of(x):
        return pl.ds(x * NY, NY)

    def pack(source, names, y_pack, z_pack):
        for a, name in enumerate(names[1]):
            y_pack[0, a] = source[name, pl.ds(0, NX, stride=NY), :]
            y_pack[1, a] = source[name, pl.ds(NY - 1, NX, stride=NY), :]
        for a, name in enumerate(names[2]):
            totals = [None, None, None, None]
            for x in range(NX):
                term = jnp.where(face, source[name, rows_of(x), :], 0.0)
                if x:
                    term = pltpu.roll(term, 2 * x, 1)
                totals[x % 4] = term if totals[x % 4] is None else totals[x % 4] + term
            z_pack[a] = (totals[0] + totals[1]) + (totals[2] + totals[3])

    def exchange(x_low, x_high, y_pack, z_pack, hx, hy, hz, send_sem, recv_sem):
        def remote(i, src, dst, target):
            return pltpu.make_async_remote_copy(
                src_ref=src, dst_ref=dst, send_sem=send_sem.at[i], recv_sem=recv_sem.at[i],
                device_id=target, device_id_type=MESH,
            )

        moves = [
            (macro < n_macro - 1, macro > 0, remote(0, x_high, hx.at[0], (macro + 1, tile, micro)), hx.at[0]),
            (macro > 0, macro < n_macro - 1, remote(1, x_low, hx.at[1], (macro - 1, tile, micro)), hx.at[1]),
            (has_up, has_down, remote(2, y_pack.at[1], hy.at[0], (macro, tile + 1, micro)), hy.at[0]),
            (has_down, has_up, remote(3, y_pack.at[0], hy.at[1], (macro, tile - 1, micro)), hy.at[1]),
        ]
        beside = remote(4, z_pack, hz, (macro, tile, 1 - micro))

        def start():
            for sends, _, copy, _ in moves:
                pl.when(sends)(copy.start)
            beside.start()

        def finish():
            for _, comes, copy, landing in moves:
                pl.when(comes)(copy.wait_recv)

                @pl.when(jnp.logical_not(comes))
                def _():
                    landing[...] = jnp.zeros(landing.shape, F32)

            beside.wait_recv()

        def drain():
            for sends, _, copy, _ in moves:
                pl.when(sends)(copy.wait_send)
            beside.wait_send()

        return start, finish, drain

    def slope_x(source, name, hx, a, x):
        up = source[name, rows_of(x + 1), :] if x < NX - 1 else hx[1, a]
        down = source[name, rows_of(x - 1), :] if x > 0 else hx[0, a]
        return up - down

    def slope_y(source, name, hy, a, x):
        if x < NX - 1:
            up = source[name, pl.ds(x * NY + 1, NY), :]
        else:
            up = pltpu.roll(source[name, rows_of(x), :], NY - 1, 0)
        if x > 0:
            down = source[name, pl.ds(x * NY - 1, NY), :]
        else:
            down = pltpu.roll(source[name, rows_of(x), :], 1, 0)
        up = jnp.where(last_row, hy[1, a, pl.ds(x, 1), :], up)
        return up - jnp.where(first_row, hy[0, a, pl.ds(x, 1), :], down)

    def slope_z(source, name, hz, a, x):
        value, beside = source[name, rows_of(x), :], hz[a]
        if x:
            beside = pltpu.roll(beside, NZ - 2 * x, 1)
        up = pltpu.roll(jnp.where(first_lane, beside, value), NZ - 1, 1)
        return up - pltpu.roll(jnp.where(last_lane, beside, value), 1, 1)

    pack(v, ((0, 1, 2),) * 3, yp1, zp1)
    start1, finish1, drain1 = exchange(
        v.at[:, pl.ds(0, NY), :], v.at[:, pl.ds(ROWS - NY, NY), :], yp1, zp1, hx1, hy1, hz1, hs1_sem, hr1_sem
    )
    start2, finish2, drain2 = exchange(
        xp2.at[0], xp2.at[1], yp2, zp2, hx2, hy2, hz2, hs2_sem, hr2_sem
    )
    start1()

    loads[2].wait()

    def widen(t, carry):
        for a in range(3):
            nf[t, a] = nz[t, a].astype(F32) * (0.1 * SCALE)
        return carry

    lax.fori_loop(0, STEPS, widen, 0)
    for a in range(3):
        q[a] = conf[a] * SCALE

    def chunk(c):
        return pl.ds(c * 128, 128)

    def block_work(order):
        block = block_of(order, 1)
        arrive(order, block, recv1, r1_sem)
        slots = pl.ds(pl.multiple_of(block * BLOCK, BLOCK), BLOCK)
        for s in range(GROUP):
            kst[pl.ds(2 * s, 2), :] = recv1[block * GROUP + s]
        kappa = kst[...] * 0.01
        for k in range(9):
            wide = jnp.broadcast_to(kappa[:, k : k + 1], (BLOCK, 128))
            kb[k] = wide + 1.0 if k % 4 == 0 else wide

        def step(t, state):
            new = []
            for c in range(BEADS // 128):
                q0, q1, q2 = state[3 * c : 3 * c + 3]
                pull = pltpu.reciprocal(
                    jnp.maximum(200.0 - q0 * q0 - (q1 * q1 + q2 * q2), 20.0), approx=True
                )
                for a in range(3):
                    here_q = (q0, q1, q2)[a]
                    other = [b for b in range(3) if b != a]
                    new.append(
                        (kb[4 * a] - pull) * here_q
                        + (kb[3 * a + other[0]] * (q0, q1, q2)[other[0]] + kb[3 * a + other[1]] * (q0, q1, q2)[other[1]])
                        + nf[t, a, slots, chunk(c)]
                    )
            return tuple(new)

        state = tuple(q[a, slots, chunk(c)] for c in range(BEADS // 128) for a in range(3))
        state = lax.fori_loop(0, STEPS, step, state, unroll=UNROLL)
        sums = [None] * 6
        for c in range(BEADS // 128):
            values = state[3 * c : 3 * c + 3]
            q0, q1, q2 = values
            pull = 1.0 / jnp.maximum(200.0 - (q0 * q0 + q1 * q1 + q2 * q2), 20.0)
            for a in range(3):
                conf_out[a, slots, chunk(c)] = values[a] * (1.0 / SCALE)
            pulled = [pull * value for value in values]
            for k, (a, b) in enumerate(PAIRS):
                term = pulled[a] * values[b]
                sums[k] = term if sums[k] is None else sums[k] + term
        lane16 = iota((BLOCK, 128), 1)
        stresses = jnp.zeros((BLOCK, 128), F32)
        for k, (a, b) in enumerate(PAIRS):
            mean = jnp.sum(sums[k], axis=1, keepdims=True) * (30.0 / BEADS)
            stresses = jnp.where(lane16 == k, 0.25 * (mean - (1.0 if a == b else 0.0)), stresses)
        pol[...] = stresses
        for s in range(GROUP):
            send2[block * GROUP + s] = pol[pl.ds(2 * s, 2), :]
        post(order, block, send2, recv2, s2_sem, r2_sem)

    def stress_work():
        finish1()
        for x in range(NX):
            grad = {}
            for a in range(3):
                grad[a, 0] = slope_x(v, a, hx1, a, x)
                grad[a, 1] = slope_y(v, a, hy1, a, x)
                grad[a, 2] = slope_z(v, a, hz1, a, x)
            half = visc[rows_of(x), :] * 0.5
            for k, (a, b) in enumerate(PAIRS):
                sp[k, rows_of(x), :] = half * (grad[a, b] + grad[b, a])
        for a in range(3):
            xp2[0, a] = sp[SIDE[0][a], rows_of(0), :]
            xp2[1, a] = sp[SIDE[0][a], rows_of(NX - 1), :]
        pack(sp, SIDE, yp2, zp2)
        start2()

    for order in range(NBLOCK):
        if order == STRESS_AT:
            stress_work()
        block_work(order)
    if STRESS_AT == NBLOCK:
        stress_work()

    viscous = jnp.zeros((FLAG, NZ), F32)
    for k, (a, b) in enumerate(PAIRS):
        viscous = jnp.where(lane == k, columns[9] * (columns[3 * a + b] + columns[3 * b + a]), viscous)
    vrow[...] = viscous
    row_col = lax.shift_right_logical(cell_col, 7)
    six = jnp.concatenate([row_col] * 6, axis=0)
    wide0, wide1 = iota((ROWS, ROWS), 0), iota((ROWS, ROWS), 1)
    six_row = jnp.sum(jnp.where(wide0 == wide1, six, 0), axis=0, keepdims=True)
    offset = jnp.where(wide1 < 64, NY, jnp.where(wide1 < 128, 1, 0))
    plus = jnp.where(wide0 == six_row - offset, 1.0, 0.0)
    minus = jnp.where((wide0 == six_row + offset) & (wide1 < 128), 1.0, 0.0)
    amat[...] = (plus - minus).astype(BF16)

    finish2()
    for x in range(NX):
        for a in range(3):
            total = slope_x(sp, SIDE[0][a], hx2, a, x)
            total = total + slope_y(sp, SIDE[1][a], hy2, a, x)
            total = total + slope_z(sp, SIDE[2][a], hz2, a, x)
            vel_out[a, rows_of(x), :] = v[a, rows_of(x), :] + 0.05 * total

    loads[1].wait()
    rank_copy.wait()
    for order in range(NBLOCK):
        arrive(order, block_of(order, 1), recv2, r2_sem)

    def collect(j, carry):
        prow[pl.ds(j, 1), :] = recv2[owners[j], pl.ds(ranks[0, j], 1), :]
        return carry

    lax.fori_loop(0, FLAG, collect, 0, unroll=8)
    returned = prow[...]
    flagged = vrow[...] + jnp.where(lane < 6, returned, 0.0)
    pick = (iota((8, NZ), 0) == iota((8, NZ), 1)).astype(F32).astype(BF16)
    turned = None
    for part in pieces(flagged, 3):
        term = lax.dot_general(pick, part, (((1,), (1,)), ((), ())), preferred_element_type=F32)
        turned = term if turned is None else turned + term
    fs_out[...] = turned[:6, :]

    spread = [jnp.broadcast_to(returned[:, k : k + 1] * 0.05, (FLAG, NZ)) for k in range(6)]
    for a in range(3):
        parts = []
        parts += pieces(jnp.where(here, spread[SIDE[0][a]], 0.0), 2)
        parts += pieces(jnp.where(here, spread[SIDE[1][a]], 0.0), 2)
        parts += pieces(
            jnp.where(below, spread[SIDE[2][a]], 0.0) - jnp.where(above, spread[SIDE[2][a]], 0.0), 2
        )
        vel_out[a] = vel_out[a] + dot(amat[...], jnp.concatenate(parts, axis=0))

    drain1()
    drain2()
    sent(send1, s1_sem)
    sent(send2, s2_sem)


def write_out(vel, conf, stress, vel_out, conf_out, stress_out, sem):
    copies = [
        pltpu.make_async_copy(source, target, sem.at[i])
        for i, (source, target) in enumerate(((conf, conf_out), (vel, vel_out), (stress, stress_out)))
    ]
    for copy in copies:
        copy.start()
    for copy in copies:
        copy.wait()


def shards(sizes, velocity, viscosity, flag_cell, flag_owner, conformations, increments):
    owner = flag_owner.reshape(FLAG)
    hbm = pl.BlockSpec(memory_space=pl.ANY)
    here = pl.BlockSpec(memory_space=pltpu.VMEM)
    vmem = lambda *shape: pltpu.VMEM(shape, F32)
    scratch = [
        pltpu.SMEM((FLAG,), I32), pltpu.SMEM((FLAG,), I32),
        pltpu.VMEM((1, FLAG), I32), pltpu.SMEM((1, FLAG), I32),
        vmem(3, SLOTS, BEADS),
        pltpu.VMEM((STEPS, 3, SLOTS, BEADS), BF16), vmem(STEPS, 3, SLOTS, BEADS),
        vmem(10, FLAG, NZ), vmem(FLAG, NZ), vmem(FLAG, NZ),
        vmem(BLOCK, 128), vmem(9, BLOCK, 128), vmem(BLOCK, 128),
        vmem(32, 2, 128), vmem(32, 2, 128), vmem(32, 2, 128), vmem(32, 2, 128),
        vmem(2, 3, NX, NZ), vmem(3, NY, NZ), vmem(2, 3, NY, NZ), vmem(2, 3, NX, NZ), vmem(3, NY, NZ),
        vmem(6, ROWS, NZ),
        vmem(2, 3, NY, NZ), vmem(2, 3, NX, NZ), vmem(3, NY, NZ),
        vmem(2, 3, NY, NZ), vmem(2, 3, NX, NZ), vmem(3, NY, NZ),
        pltpu.VMEM((ROWS, ROWS), BF16),
        pltpu.SemaphoreType.DMA((4,)),
        pltpu.SemaphoreType.DMA, pltpu.SemaphoreType.DMA((NBLOCK,)),
        pltpu.SemaphoreType.DMA, pltpu.SemaphoreType.DMA((NBLOCK,)),
        pltpu.SemaphoreType.DMA((5,)), pltpu.SemaphoreType.DMA((5,)),
        pltpu.SemaphoreType.DMA((5,)), pltpu.SemaphoreType.DMA((5,)),
    ]
    shapes = (
        jax.ShapeDtypeStruct((3, ROWS, NZ), F32),
        jax.ShapeDtypeStruct(conformations.shape, F32),
        jax.ShapeDtypeStruct((6, FLAG), F32),
    )
    results = pl.pallas_call(
        functools.partial(kernel, *sizes),
        out_shape=shapes,
        in_specs=[here, here, hbm, here, hbm, here, here, hbm],
        out_specs=(here, here, here),
        scratch_shapes=scratch,
        compiler_params=pltpu.CompilerParams(
            collective_id=0, has_side_effects=True, vmem_limit_bytes=52 * 2**20
        ),
    )(
        velocity.reshape(3, ROWS, NZ), viscosity.reshape(ROWS, NZ),
        flag_cell, flag_cell.reshape(1, FLAG), owner, owner.reshape(1, FLAG),
        conformations, increments,
    )
    vel, conf, stress = pl.pallas_call(
        write_out,
        out_shape=shapes,
        in_specs=[here] * 3,
        out_specs=(hbm,) * 3,
        scratch_shapes=[pltpu.SemaphoreType.DMA((3,))],
        compiler_params=pltpu.CompilerParams(vmem_limit_bytes=4 * 2**20),
    )(*results)
    return vel.reshape(velocity.shape), conf, stress


def solution(mesh):
    sizes = (mesh.shape["macro"], mesh.shape["tile"], mesh.shape["micro"])
    in_specs = (
        P(None, "macro", "tile", "micro"),
        P("macro", "tile", "micro"),
        P(("macro", "tile", "micro")),
        P(("macro", "tile", "micro"), None),
        P(None, ("macro", "tile", "micro"), None),
        P(None, None, ("macro", "tile", "micro"), None),
    )
    out_specs = (
        P(None, "macro", "tile", "micro"),
        P(None, ("macro", "tile", "micro"), None),
        P(None, ("macro", "tile", "micro")),
    )
    return jax.shard_map(
        functools.partial(shards, sizes), mesh=mesh, in_specs=in_specs, out_specs=out_specs, check_vma=False
    )
```

```python
import functools
import math

import jax
import jax.numpy as jnp
from jax import lax
from jax.experimental import pallas as pl
from jax.experimental.pallas import tpu as pltpu
from jax.sharding import PartitionSpec as P

MESH = pl.DeviceIdType.MESH
F32, BF16, I32 = jnp.float32, jnp.bfloat16, jnp.int32

PAIRS = ((0, 0), (1, 1), (2, 2), (0, 1), (0, 2), (1, 2))
SIDE = ((0, 3, 4), (3, 1, 5), (4, 5, 2))
SCALE = math.sqrt(200.0 / 30.0)

NX, NY, NZ = 24, 8, 128
ROWS = NX * NY
FLAG = 32
SLOTS = 64
BEADS = 512
STEPS = 16
BLOCK = 16
GROUP = BLOCK // 2
NBLOCK = SLOTS // BLOCK
STRESS_AT = 2
UNROLL = 4


def iota(shape, dim):
    return lax.broadcasted_iota(I32, shape, dim)


def pieces(x, count):
    out = []
    for _ in range(count):
        part = x.astype(BF16)
        out.append(part)
        x = x - part.astype(F32)
    return out


def column(row):
    diagonal = iota((FLAG, FLAG), 0) == iota((FLAG, FLAG), 1)
    return jnp.sum(jnp.where(diagonal, row, 0), axis=1, keepdims=True)


def dot(a, b):
    return jnp.dot(a, b, preferred_element_type=F32)


def kernel(
    n_macro, n_tile, n_micro,
    v_in, visc_in, cells_in, cell_in, owner_in, conf_in, noise_in,
    vel_out, conf_out, recv2, amat_out, vrow_out, rank_out,
    v, visc, cells, cellv, ownerv, rankv, q, nz, nf, gat, vrow, vel,
    kst, kb, pol, send1, recv1, send2,
    yp1, zp1, hx1, hy1, hz1, sp, xp2, yp2, zp2, hx2, hy2, hz2, amat,
    in_sem, out_sem, s1_sem, r1_sem, s2_sem, r2_sem, hs1_sem, hr1_sem, hs2_sem, hr2_sem,
):
    macro, tile, micro = lax.axis_index("macro"), lax.axis_index("tile"), lax.axis_index("micro")
    owners_n = n_macro * n_micro
    me = macro * n_micro + micro
    my_block = lax.div(me, GROUP)

    loads = [
        pltpu.make_async_copy(v_in, v, in_sem.at[0]),
        pltpu.make_async_copy(cells_in, cells, in_sem.at[1]),
        pltpu.make_async_copy(cell_in, cellv, in_sem.at[2]),
        pltpu.make_async_copy(owner_in, ownerv, in_sem.at[3]),
        pltpu.make_async_copy(visc_in, visc, in_sem.at[4]),
        pltpu.make_async_copy(noise_in, nz, in_sem.at[5]),
        pltpu.make_async_copy(conf_in, q, in_sem.at[6]),
    ]
    for load in loads:
        load.start()

    barrier = pltpu.get_barrier_semaphore()
    has_up, has_down = tile < n_tile - 1, tile > 0

    def peer_id(peer):
        return (lax.div(peer, n_micro), tile, lax.rem(peer, n_micro))

    def greet(k, carry):
        pl.semaphore_signal(
            barrier, inc=1, device_id=peer_id(lax.rem(me + k, owners_n)), device_id_type=MESH
        )
        return carry

    lax.fori_loop(1, owners_n, greet, 0, unroll=True)

    @pl.when(has_up)
    def _():
        pl.semaphore_signal(barrier, inc=1, device_id=(macro, tile + 1, micro), device_id_type=MESH)

    @pl.when(has_down)
    def _():
        pl.semaphore_signal(barrier, inc=1, device_id=(macro, tile - 1, micro), device_id_type=MESH)

    for load in loads[:5]:
        load.wait()

    def gather(j, carry):
        row = lax.shift_right_logical(cells[j], 7)
        row = jnp.minimum(jnp.maximum(row, NY), ROWS - NY - 1)
        for a in range(3):
            read = lambda offset: v[a, pl.ds(row + offset, 1), :]
            gat[3 * a, pl.ds(j, 1), :] = read(NY) - read(-NY)
            gat[3 * a + 1, pl.ds(j, 1), :] = read(1) - read(-1)
            gat[3 * a + 2, pl.ds(j, 1), :] = read(0)
        gat[9, pl.ds(j, 1), :] = visc[pl.ds(row, 1), :]
        return carry

    lax.fori_loop(0, FLAG, gather, 0, unroll=8)

    square0, square1 = iota((FLAG, FLAG), 0), iota((FLAG, FLAG), 1)
    cell_row, owner_row = cellv[...], ownerv[...]
    cell_col, owner_col = column(cell_row), column(owner_row)
    z_col = cell_col & (NZ - 1)
    lane = iota((FLAG, NZ), 1)
    here, above, below = lane == z_col, lane == z_col + 1, lane == z_col - 1
    rank_row = jnp.sum(
        jnp.where((square0 < square1) & (owner_col == owner_row), 1, 0), axis=0, keepdims=True
    )
    rankv[...] = jnp.minimum(rank_row, 1)
    rank_copy = pltpu.make_async_copy(rankv, rank_out, out_sem.at[0])
    rank_copy.start()

    gathered = jnp.zeros((FLAG, NZ), F32)
    columns = []
    for k in range(10):
        values = gat[k]
        if k < 9 and k % 3 == 2:
            picked = jnp.where(above, values, 0.0) - jnp.where(below, values, 0.0)
        else:
            picked = jnp.where(here, values, 0.0)
        if k < 9:
            picked = picked * 0.5
        columns.append(jnp.sum(picked, axis=1, keepdims=True))
        if k < 9:
            gathered = jnp.where(lane == k, columns[k], gathered)
    position = owner_row * 2 + rank_row
    placing = (iota((SLOTS, FLAG), 0) == position).astype(F32).astype(BF16)
    hi, mid, lo = pieces(gathered, 3)
    outgoing = dot(placing, hi) + (dot(placing, mid) + dot(placing, lo))
    for s in range(owners_n):
        send1[s] = outgoing[2 * s : 2 * s + 2, :]

    @pl.when(has_up & has_down)
    def _():
        pl.semaphore_wait(barrier, owners_n + 1)

    @pl.when(jnp.logical_not(has_up & has_down))
    def _():
        pl.semaphore_wait(barrier, owners_n)

    def block_of(order, sign):
        shift = (0, 1, NBLOCK - 1, 2)[order]
        return lax.rem(my_block + sign * shift + NBLOCK, NBLOCK)

    def post(order, block, send, recv, send_sem, recv_sem, own):
        if order == 0:
            own(me)
        base = block * GROUP
        turn = me - my_block * GROUP
        for k in range(1 if order == 0 else 0, GROUP):
            peer = base + lax.rem(turn + k, GROUP)
            pltpu.make_async_remote_copy(
                src_ref=send.at[peer], dst_ref=recv.at[me],
                send_sem=send_sem, recv_sem=recv_sem.at[my_block],
                device_id=peer_id(peer), device_id_type=MESH,
            ).start()

    def arrive(order, block, recv, recv_sem):
        part = recv.at[pl.ds(0, GROUP - 1 if order == 0 else GROUP)]
        pltpu.make_async_copy(part, part, recv_sem.at[block]).wait()

    def sent(send, send_sem):
        part = send.at[pl.ds(0, owners_n - 1)]
        pltpu.make_async_copy(part, part, send_sem).wait()

    def keep_row(i):
        recv1[i] = send1[i]

    def own_row(i):
        return pltpu.make_async_copy(send2.at[i], recv2.at[i], out_sem.at[1])

    for order in range(NBLOCK):
        post(order, block_of(order, -1), send1, recv1, s1_sem, r1_sem, keep_row)

    sub, lanes = iota((NY, NZ), 0), iota((NY, NZ), 1)
    face = lanes == jnp.where(micro == 0, NZ - 1, 0)
    first_lane, last_lane = lanes == 0, lanes == NZ - 1
    first_row, last_row = sub == 0, sub == NY - 1

    def rows_of(x):
        return pl.ds(x * NY, NY)

    def pack(source, names, y_pack, z_pack):
        for a, name in enumerate(names[1]):
            y_pack[0, a] = source[name, pl.ds(0, NX, stride=NY), :]
            y_pack[1, a] = source[name, pl.ds(NY - 1, NX, stride=NY), :]
        for a, name in enumerate(names[2]):
            totals = [None, None, None, None]
            for x in range(NX):
                term = jnp.where(face, source[name, rows_of(x), :], 0.0)
                if x:
                    term = pltpu.roll(term, 2 * x, 1)
                totals[x % 4] = term if totals[x % 4] is None else totals[x % 4] + term
            z_pack[a] = (totals[0] + totals[1]) + (totals[2] + totals[3])

    def exchange(x_low, x_high, y_pack, z_pack, hx, hy, hz, send_sem, recv_sem):
        def remote(i, src, dst, target):
            return pltpu.make_async_remote_copy(
                src_ref=src, dst_ref=dst, send_sem=send_sem.at[i], recv_sem=recv_sem.at[i],
                device_id=target, device_id_type=MESH,
            )

        moves = [
            (macro < n_macro - 1, macro > 0, remote(0, x_high, hx.at[0], (macro + 1, tile, micro)), hx.at[0]),
            (macro > 0, macro < n_macro - 1, remote(1, x_low, hx.at[1], (macro - 1, tile, micro)), hx.at[1]),
            (has_up, has_down, remote(2, y_pack.at[1], hy.at[0], (macro, tile + 1, micro)), hy.at[0]),
            (has_down, has_up, remote(3, y_pack.at[0], hy.at[1], (macro, tile - 1, micro)), hy.at[1]),
        ]
        beside = remote(4, z_pack, hz, (macro, tile, 1 - micro))

        def start():
            for sends, _, copy, _ in moves:
                pl.when(sends)(copy.start)
            beside.start()

        def finish():
            for _, comes, copy, landing in moves:
                pl.when(comes)(copy.wait_recv)

                @pl.when(jnp.logical_not(comes))
                def _():
                    landing[...] = jnp.zeros(landing.shape, F32)

            beside.wait_recv()

        def drain():
            for sends, _, copy, _ in moves:
                pl.when(sends)(copy.wait_send)
            beside.wait_send()

        return start, finish, drain

    def slope_x(source, name, hx, a, x):
        up = source[name, rows_of(x + 1), :] if x < NX - 1 else hx[1, a]
        down = source[name, rows_of(x - 1), :] if x > 0 else hx[0, a]
        return up - down

    def slope_y(source, name, hy, a, x):
        if x < NX - 1:
            up = source[name, pl.ds(x * NY + 1, NY), :]
        else:
            up = pltpu.roll(source[name, rows_of(x), :], NY - 1, 0)
        if x > 0:
            down = source[name, pl.ds(x * NY - 1, NY), :]
        else:
            down = pltpu.roll(source[name, rows_of(x), :], 1, 0)
        up = jnp.where(last_row, hy[1, a, pl.ds(x, 1), :], up)
        return up - jnp.where(first_row, hy[0, a, pl.ds(x, 1), :], down)

    def slope_z(source, name, hz, a, x):
        value, beside = source[name, rows_of(x), :], hz[a]
        if x:
            beside = pltpu.roll(beside, NZ - 2 * x, 1)
        up = pltpu.roll(jnp.where(first_lane, beside, value), NZ - 1, 1)
        return up - pltpu.roll(jnp.where(last_lane, beside, value), 1, 1)

    pack(v, ((0, 1, 2),) * 3, yp1, zp1)
    start1, finish1, drain1 = exchange(
        v.at[:, pl.ds(0, NY), :], v.at[:, pl.ds(ROWS - NY, NY), :], yp1, zp1, hx1, hy1, hz1, hs1_sem, hr1_sem
    )
    start2, finish2, drain2 = exchange(
        xp2.at[0], xp2.at[1], yp2, zp2, hx2, hy2, hz2, hs2_sem, hr2_sem
    )
    start1()

    loads[5].wait()

    def widen(t, carry):
        for a in range(3):
            nf[t, a] = nz[t, a].astype(F32) * (0.1 * SCALE)
        return carry

    lax.fori_loop(0, STEPS, widen, 0)
    loads[6].wait()
    for a in range(3):
        q[a] = q[a] * SCALE

    def chunk(c):
        return pl.ds(c * 128, 128)

    def block_work(order):
        block = block_of(order, 1)
        arrive(order, block, recv1, r1_sem)
        slots = pl.ds(pl.multiple_of(block * BLOCK, BLOCK), BLOCK)
        for s in range(GROUP):
            kst[pl.ds(2 * s, 2), :] = recv1[block * GROUP + s]
        kappa = kst[...] * 0.01
        for k in range(9):
            wide = jnp.broadcast_to(kappa[:, k : k + 1], (BLOCK, 128))
            kb[k] = wide + 1.0 if k % 4 == 0 else wide

        def step(t, state):
            new = []
            for c in range(BEADS // 128):
                q0, q1, q2 = state[3 * c : 3 * c + 3]
                pull = pltpu.reciprocal(
                    jnp.maximum(200.0 - q0 * q0 - (q1 * q1 + q2 * q2), 20.0), approx=True
                )
                for a in range(3):
                    here_q = (q0, q1, q2)[a]
                    other = [b for b in range(3) if b != a]
                    new.append(
                        (kb[4 * a] - pull) * here_q
                        + (kb[3 * a + other[0]] * (q0, q1, q2)[other[0]] + kb[3 * a + other[1]] * (q0, q1, q2)[other[1]])
                        + nf[t, a, slots, chunk(c)]
                    )
            return tuple(new)

        state = tuple(q[a, slots, chunk(c)] for c in range(BEADS // 128) for a in range(3))
        state = lax.fori_loop(0, STEPS, step, state, unroll=UNROLL)
        sums = [None] * 6
        for c in range(BEADS // 128):
            values = state[3 * c : 3 * c + 3]
            q0, q1, q2 = values
            pull = 1.0 / jnp.maximum(200.0 - (q0 * q0 + q1 * q1 + q2 * q2), 20.0)
            for a in range(3):
                q[a, slots, chunk(c)] = values[a] * (1.0 / SCALE)
            pulled = [pull * value for value in values]
            for k, (a, b) in enumerate(PAIRS):
                term = pulled[a] * values[b]
                sums[k] = term if sums[k] is None else sums[k] + term
        lane16 = iota((BLOCK, 128), 1)
        stresses = jnp.zeros((BLOCK, 128), F32)
        for k, (a, b) in enumerate(PAIRS):
            mean = jnp.sum(sums[k], axis=1, keepdims=True) * (30.0 / BEADS)
            stresses = jnp.where(lane16 == k, 0.25 * (mean - (1.0 if a == b else 0.0)), stresses)
        pol[...] = stresses
        for s in range(GROUP):
            send2[block * GROUP + s] = pol[pl.ds(2 * s, 2), :]
        post(order, block, send2, recv2, s2_sem, r2_sem, lambda i: own_row(i).start())

    def stress_work():
        finish1()
        for x in range(NX):
            grad = {}
            for a in range(3):
                grad[a, 0] = slope_x(v, a, hx1, a, x)
                grad[a, 1] = slope_y(v, a, hy1, a, x)
                grad[a, 2] = slope_z(v, a, hz1, a, x)
            half = visc[rows_of(x), :] * 0.5
            for k, (a, b) in enumerate(PAIRS):
                sp[k, rows_of(x), :] = half * (grad[a, b] + grad[b, a])
        for a in range(3):
            xp2[0, a] = sp[SIDE[0][a], rows_of(0), :]
            xp2[1, a] = sp[SIDE[0][a], rows_of(NX - 1), :]
        pack(sp, SIDE, yp2, zp2)
        start2()

    for order in range(NBLOCK):
        if order == STRESS_AT:
            stress_work()
        block_work(order)
    if STRESS_AT == NBLOCK:
        stress_work()

    viscous = jnp.zeros((FLAG, NZ), F32)
    for k, (a, b) in enumerate(PAIRS):
        viscous = jnp.where(lane == k, columns[9] * (columns[3 * a + b] + columns[3 * b + a]), viscous)
    vrow[...] = viscous
    vrow_copy = pltpu.make_async_copy(vrow, vrow_out, out_sem.at[2])
    vrow_copy.start()
    row_col = lax.shift_right_logical(cell_col, 7)
    six = jnp.concatenate([row_col] * 6, axis=0)
    wide0, wide1 = iota((ROWS, ROWS), 0), iota((ROWS, ROWS), 1)
    six_row = jnp.sum(jnp.where(wide0 == wide1, six, 0), axis=0, keepdims=True)
    offset = jnp.where(wide1 < 64, NY, jnp.where(wide1 < 128, 1, 0))
    plus = jnp.where(wide0 == six_row - offset, 1.0, 0.0)
    minus = jnp.where((wide0 == six_row + offset) & (wide1 < 128), 1.0, 0.0)
    amat[...] = (plus - minus).astype(BF16)
    amat_copy = pltpu.make_async_copy(amat, amat_out, out_sem.at[3])
    amat_copy.start()
    conf_copy = pltpu.make_async_copy(q, conf_out, out_sem.at[4])
    conf_copy.start()

    finish2()
    for x in range(NX):
        for a in range(3):
            total = slope_x(sp, SIDE[0][a], hx2, a, x)
            total = total + slope_y(sp, SIDE[1][a], hy2, a, x)
            total = total + slope_z(sp, SIDE[2][a], hz2, a, x)
            vel[a, rows_of(x), :] = v[a, rows_of(x), :] + 0.05 * total

    vel_copy = pltpu.make_async_copy(vel, vel_out, out_sem.at[5])
    vel_copy.start()

    drain1()
    drain2()
    sent(send1, s1_sem)
    sent(send2, s2_sem)
    for copy in (rank_copy, vrow_copy, amat_copy, conf_copy, vel_copy, own_row(me)):
        copy.wait()
    for order in range(NBLOCK):
        arrive(order, block_of(order, 1), recv2, r2_sem)


def finish(
    vel_in, conf_in, back_in, amat_in, vrow_in, rank_in, cell_in, owners_in,
    vel_out, conf_out, fs_out,
    conf, vel, back, amat, vrow, ranks, cellv, owners, prow, stress, in_sem, out_sem,
):
    loads = [
        pltpu.make_async_copy(source, target, in_sem.at[i])
        for i, (source, target) in enumerate(
            (
                (back_in, back), (rank_in, ranks), (owners_in, owners), (cell_in, cellv),
                (vrow_in, vrow), (amat_in, amat), (vel_in, vel), (conf_in, conf),
            )
        )
    ]
    for load in loads:
        load.start()
    for load in loads[:5]:
        load.wait()

    def collect(j, carry):
        prow[pl.ds(j, 1), :] = back[owners[j], pl.ds(ranks[0, j], 1), :]
        return carry

    lax.fori_loop(0, FLAG, collect, 0, unroll=True)
    lane = iota((FLAG, NZ), 1)
    z_col = column(cellv[...]) & (NZ - 1)
    here, above, below = lane == z_col, lane == z_col + 1, lane == z_col - 1
    returned = prow[...]
    flagged = vrow[...] + jnp.where(lane < 6, returned, 0.0)
    pick = (iota((8, NZ), 0) == iota((8, NZ), 1)).astype(F32).astype(BF16)
    turned = None
    for part in pieces(flagged, 3):
        term = lax.dot_general(pick, part, (((1,), (1,)), ((), ())), preferred_element_type=F32)
        turned = term if turned is None else turned + term
    stress[...] = turned[:6, :]
    stress_copy = pltpu.make_async_copy(stress, fs_out, out_sem.at[1])
    stress_copy.start()

    spread = [jnp.broadcast_to(returned[:, k : k + 1] * 0.05, (FLAG, NZ)) for k in range(6)]
    loads[7].wait()
    conf_copy = pltpu.make_async_copy(conf, conf_out, out_sem.at[0])
    conf_copy.start()
    for load in loads[5:7]:
        load.wait()
    for a in range(3):
        parts = []
        parts += pieces(jnp.where(here, spread[SIDE[0][a]], 0.0), 2)
        parts += pieces(jnp.where(here, spread[SIDE[1][a]], 0.0), 2)
        parts += pieces(
            jnp.where(below, spread[SIDE[2][a]], 0.0) - jnp.where(above, spread[SIDE[2][a]], 0.0), 2
        )
        vel[a] = vel[a] + dot(amat[...], jnp.concatenate(parts, axis=0))
        pltpu.make_async_copy(vel.at[a], vel_out.at[a], out_sem.at[2]).start()
    conf_copy.wait()
    stress_copy.wait()
    pltpu.make_async_copy(vel, vel_out, out_sem.at[2]).wait()


def shards(sizes, velocity, viscosity, flag_cell, flag_owner, conformations, increments):
    owner = flag_owner.reshape(FLAG)
    cell_row, owner_row = flag_cell.reshape(1, FLAG), flag_owner.reshape(1, FLAG)
    hbm = pl.BlockSpec(memory_space=pl.ANY)
    vmem = lambda *shape: pltpu.VMEM(shape, F32)
    shape = jax.ShapeDtypeStruct
    scratch = [
        vmem(3, ROWS, NZ), vmem(ROWS, NZ),
        pltpu.SMEM((FLAG,), I32), pltpu.VMEM((1, FLAG), I32), pltpu.VMEM((1, FLAG), I32), pltpu.VMEM((1, FLAG), I32),
        vmem(3, SLOTS, BEADS),
        pltpu.VMEM((STEPS, 3, SLOTS, BEADS), BF16), vmem(STEPS, 3, SLOTS, BEADS),
        vmem(10, FLAG, NZ), vmem(FLAG, NZ), vmem(3, ROWS, NZ),
        vmem(BLOCK, 128), vmem(9, BLOCK, 128), vmem(BLOCK, 128),
        vmem(32, 2, 128), vmem(32, 2, 128), vmem(32, 2, 128),
        vmem(2, 3, NX, NZ), vmem(3, NY, NZ), vmem(2, 3, NY, NZ), vmem(2, 3, NX, NZ), vmem(3, NY, NZ),
        vmem(6, ROWS, NZ),
        vmem(2, 3, NY, NZ), vmem(2, 3, NX, NZ), vmem(3, NY, NZ),
        vmem(2, 3, NY, NZ), vmem(2, 3, NX, NZ), vmem(3, NY, NZ),
        pltpu.VMEM((ROWS, ROWS), BF16),
        pltpu.SemaphoreType.DMA((7,)), pltpu.SemaphoreType.DMA((6,)),
        pltpu.SemaphoreType.DMA, pltpu.SemaphoreType.DMA((NBLOCK,)),
        pltpu.SemaphoreType.DMA, pltpu.SemaphoreType.DMA((NBLOCK,)),
        pltpu.SemaphoreType.DMA((5,)), pltpu.SemaphoreType.DMA((5,)),
        pltpu.SemaphoreType.DMA((5,)), pltpu.SemaphoreType.DMA((5,)),
    ]
    vel, conf = shape((3, ROWS, NZ), F32), shape(conformations.shape, F32)
    held = pl.pallas_call(
        functools.partial(kernel, *sizes),
        out_shape=(
            vel, conf, shape((32, 2, 128), F32), shape((ROWS, ROWS), BF16), shape((FLAG, NZ), F32),
            shape((1, FLAG), I32),
        ),
        in_specs=[hbm] * 7,
        out_specs=(hbm,) * 6,
        scratch_shapes=scratch,
        compiler_params=pltpu.CompilerParams(
            collective_id=0, has_side_effects=True, vmem_limit_bytes=56 * 2**20
        ),
    )(
        velocity.reshape(3, ROWS, NZ), viscosity.reshape(ROWS, NZ),
        flag_cell, cell_row, owner_row, conformations, increments,
    )
    vel, conf, stress = pl.pallas_call(
        finish,
        out_shape=(vel, conf, shape((6, FLAG), F32)),
        in_specs=[hbm] * 8,
        out_specs=(hbm,) * 3,
        scratch_shapes=[
            vmem(3, SLOTS, BEADS), vmem(3, ROWS, NZ), vmem(32, 2, 128), pltpu.VMEM((ROWS, ROWS), BF16), vmem(FLAG, NZ),
            pltpu.SMEM((1, FLAG), I32), pltpu.VMEM((1, FLAG), I32), pltpu.SMEM((FLAG,), I32),
            vmem(FLAG, NZ), vmem(6, FLAG),
            pltpu.SemaphoreType.DMA((8,)), pltpu.SemaphoreType.DMA((3,)),
        ],
        compiler_params=pltpu.CompilerParams(vmem_limit_bytes=56 * 2**20),
    )(*held, cell_row, owner)
    return vel.reshape(velocity.shape), conf, stress


def solution(mesh):
    sizes = (mesh.shape["macro"], mesh.shape["tile"], mesh.shape["micro"])
    in_specs = (
        P(None, "macro", "tile", "micro"),
        P("macro", "tile", "micro"),
        P(("macro", "tile", "micro")),
        P(("macro", "tile", "micro"), None),
        P(None, ("macro", "tile", "micro"), None),
        P(None, None, ("macro", "tile", "micro"), None),
    )
    out_specs = (
        P(None, "macro", "tile", "micro"),
        P(None, ("macro", "tile", "micro"), None),
        P(None, ("macro", "tile", "micro")),
    )
    return jax.shard_map(
        functools.partial(shards, sizes), mesh=mesh, in_specs=in_specs, out_specs=out_specs, check_vma=False
    )
```

```python
import functools
import math

import jax
import jax.numpy as jnp
from jax import lax
from jax.experimental import pallas as pl
from jax.experimental.pallas import tpu as pltpu
from jax.sharding import PartitionSpec as P

MESH = pl.DeviceIdType.MESH
F32, BF16, I32 = jnp.float32, jnp.bfloat16, jnp.int32

PAIRS = ((0, 0), (1, 1), (2, 2), (0, 1), (0, 2), (1, 2))
SIDE = ((0, 3, 4), (3, 1, 5), (4, 5, 2))
SCALE = math.sqrt(200.0 / 30.0)

NX, NY, NZ = 24, 8, 128
ROWS = NX * NY
FLAG = 32
SLOTS = 64
BEADS = 512
STEPS = 16
BLOCK = 16
GROUP = BLOCK // 2
NBLOCK = SLOTS // BLOCK
STRESS_AT = 1
UNROLL = 8


def iota(shape, dim):
    return lax.broadcasted_iota(I32, shape, dim)


def pieces(x, count):
    out = []
    for _ in range(count):
        part = x.astype(BF16)
        out.append(part)
        x = x - part.astype(F32)
    return out


def column(row):
    diagonal = iota((FLAG, FLAG), 0) == iota((FLAG, FLAG), 1)
    return jnp.sum(jnp.where(diagonal, row, 0), axis=1, keepdims=True)


def dot(a, b):
    return jnp.dot(a, b, preferred_element_type=F32)


def kernel(
    n_macro, n_tile, n_micro,
    v_in, visc_in, cells_in, cell_in, owner_in, conf_in, noise_in,
    vel_out, conf_out, recv2, amat_out, vrow_out, rank_out,
    v, visc, cells, cellv, ownerv, rankv, q, nz, nf, gat, vrow, vel,
    kst, kb, pol, send1, recv1, send2,
    yp1, zp1, hx1, hy1, hz1, sp, xp2, yp2, zp2, hx2, hy2, hz2, amat, layers,
    in_sem, out_sem, s1_sem, r1_sem, s2_sem, r2_sem, hs1_sem, hr1_sem, hs2_sem, hr2_sem,
):
    macro, tile, micro = lax.axis_index("macro"), lax.axis_index("tile"), lax.axis_index("micro")
    owners_n = n_macro * n_micro
    me = macro * n_micro + micro
    my_block = lax.div(me, GROUP)

    loads = [
        pltpu.make_async_copy(v_in, v, in_sem.at[0]),
        pltpu.make_async_copy(cells_in, cells, in_sem.at[1]),
        pltpu.make_async_copy(cell_in, cellv, in_sem.at[2]),
        pltpu.make_async_copy(owner_in, ownerv, in_sem.at[3]),
        pltpu.make_async_copy(visc_in, visc, in_sem.at[4]),
        pltpu.make_async_copy(noise_in, nz, in_sem.at[5]),
        pltpu.make_async_copy(conf_in, q, in_sem.at[6]),
    ]
    for load in loads:
        load.start()

    barrier = pltpu.get_barrier_semaphore()
    has_up, has_down = tile < n_tile - 1, tile > 0

    def peer_id(peer):
        return (lax.div(peer, n_micro), tile, lax.rem(peer, n_micro))

    def greet(k, carry):
        pl.semaphore_signal(
            barrier, inc=1, device_id=peer_id(lax.rem(me + k, owners_n)), device_id_type=MESH
        )
        return carry

    lax.fori_loop(1, owners_n, greet, 0, unroll=True)

    @pl.when(has_up)
    def _():
        pl.semaphore_signal(barrier, inc=1, device_id=(macro, tile + 1, micro), device_id_type=MESH)

    @pl.when(has_down)
    def _():
        pl.semaphore_signal(barrier, inc=1, device_id=(macro, tile - 1, micro), device_id_type=MESH)

    for load in loads[:5]:
        load.wait()

    def gather(j, carry):
        row = lax.shift_right_logical(cells[j], 7)
        row = jnp.minimum(jnp.maximum(row, NY), ROWS - NY - 1)
        for a in range(3):
            read = lambda offset: v[a, pl.ds(row + offset, 1), :]
            gat[3 * a, pl.ds(j, 1), :] = read(NY) - read(-NY)
            gat[3 * a + 1, pl.ds(j, 1), :] = read(1) - read(-1)
            gat[3 * a + 2, pl.ds(j, 1), :] = read(0)
        gat[9, pl.ds(j, 1), :] = visc[pl.ds(row, 1), :]
        return carry

    lax.fori_loop(0, FLAG, gather, 0, unroll=8)

    square0, square1 = iota((FLAG, FLAG), 0), iota((FLAG, FLAG), 1)
    cell_row, owner_row = cellv[...], ownerv[...]
    cell_col, owner_col = column(cell_row), column(owner_row)
    z_col = cell_col & (NZ - 1)
    lane = iota((FLAG, NZ), 1)
    here, above, below = lane == z_col, lane == z_col + 1, lane == z_col - 1
    rank_row = jnp.sum(
        jnp.where((square0 < square1) & (owner_col == owner_row), 1, 0), axis=0, keepdims=True
    )
    rankv[...] = jnp.minimum(rank_row, 1)
    rank_copy = pltpu.make_async_copy(rankv, rank_out, out_sem.at[0])
    rank_copy.start()

    gathered = jnp.zeros((FLAG, NZ), F32)
    columns = []
    for k in range(10):
        values = gat[k]
        if k < 9 and k % 3 == 2:
            picked = jnp.where(above, values, 0.0) - jnp.where(below, values, 0.0)
        else:
            picked = jnp.where(here, values, 0.0)
        if k < 9:
            picked = picked * 0.5
        columns.append(jnp.sum(picked, axis=1, keepdims=True))
        if k < 9:
            gathered = jnp.where(lane == k, columns[k], gathered)
    position = owner_row * 2 + rank_row
    placing = (iota((SLOTS, FLAG), 0) == position).astype(F32).astype(BF16)
    hi, mid, lo = pieces(gathered, 3)
    outgoing = dot(placing, hi) + (dot(placing, mid) + dot(placing, lo))
    for s in range(owners_n):
        send1[s] = outgoing[2 * s : 2 * s + 2, :]

    @pl.when(has_up & has_down)
    def _():
        pl.semaphore_wait(barrier, owners_n + 1)

    @pl.when(jnp.logical_not(has_up & has_down))
    def _():
        pl.semaphore_wait(barrier, owners_n)

    def block_of(order, sign):
        shift = (0, 1, NBLOCK - 1, 2)[order]
        return lax.rem(my_block + sign * shift + NBLOCK, NBLOCK)

    def post(order, block, send, recv, send_sem, recv_sem, own):
        if order == 0:
            own(me)
        base = block * GROUP
        turn = me - my_block * GROUP
        for k in range(1 if order == 0 else 0, GROUP):
            peer = base + lax.rem(turn + k, GROUP)
            pltpu.make_async_remote_copy(
                src_ref=send.at[peer], dst_ref=recv.at[me],
                send_sem=send_sem, recv_sem=recv_sem.at[my_block],
                device_id=peer_id(peer), device_id_type=MESH,
            ).start()

    def arrive(order, block, recv, recv_sem):
        part = recv.at[pl.ds(0, GROUP - 1 if order == 0 else GROUP)]
        pltpu.make_async_copy(part, part, recv_sem.at[block]).wait()

    def sent(send, send_sem):
        part = send.at[pl.ds(0, owners_n - 1)]
        pltpu.make_async_copy(part, part, send_sem).wait()

    def keep_row(i):
        recv1[i] = send1[i]

    def own_row(i):
        return pltpu.make_async_copy(send2.at[i], recv2.at[i], out_sem.at[1])

    for order in range(NBLOCK):
        post(order, block_of(order, -1), send1, recv1, s1_sem, r1_sem, keep_row)

    sub, lanes = iota((NY, NZ), 0), iota((NY, NZ), 1)
    face = lanes == jnp.where(micro == 0, NZ - 1, 0)
    first_lane, last_lane = lanes == 0, lanes == NZ - 1
    first_row, last_row = sub == 0, sub == NY - 1

    def rows_of(x):
        return pl.ds(x * NY, NY)

    def pack(source, names, y_pack, z_pack):
        for a, name in enumerate(names[1]):
            y_pack[0, a] = source[name, pl.ds(0, NX, stride=NY), :]
            y_pack[1, a] = source[name, pl.ds(NY - 1, NX, stride=NY), :]
        for a, name in enumerate(names[2]):
            totals = [None, None, None, None]
            for x in range(NX):
                term = jnp.where(face, source[name, rows_of(x), :], 0.0)
                if x:
                    term = pltpu.roll(term, 2 * x, 1)
                totals[x % 4] = term if totals[x % 4] is None else totals[x % 4] + term
            z_pack[a] = (totals[0] + totals[1]) + (totals[2] + totals[3])

    def exchange(x_low, x_high, y_pack, z_pack, hx, hy, hz, send_sem, recv_sem):
        def remote(i, src, dst, target):
            return pltpu.make_async_remote_copy(
                src_ref=src, dst_ref=dst, send_sem=send_sem.at[i], recv_sem=recv_sem.at[i],
                device_id=target, device_id_type=MESH,
            )

        moves = [
            (macro < n_macro - 1, macro > 0, remote(0, x_high, hx.at[0], (macro + 1, tile, micro)), hx.at[0]),
            (macro > 0, macro < n_macro - 1, remote(1, x_low, hx.at[1], (macro - 1, tile, micro)), hx.at[1]),
            (has_up, has_down, remote(2, y_pack.at[1], hy.at[0], (macro, tile + 1, micro)), hy.at[0]),
            (has_down, has_up, remote(3, y_pack.at[0], hy.at[1], (macro, tile - 1, micro)), hy.at[1]),
        ]
        beside = remote(4, z_pack, hz, (macro, tile, 1 - micro))

        def start():
            for sends, _, copy, _ in moves:
                pl.when(sends)(copy.start)
            beside.start()

        def finish():
            for _, comes, copy, landing in moves:
                pl.when(comes)(copy.wait_recv)

                @pl.when(jnp.logical_not(comes))
                def _():
                    landing[...] = jnp.zeros(landing.shape, F32)

            beside.wait_recv()

        def drain():
            for sends, _, copy, _ in moves:
                pl.when(sends)(copy.wait_send)
            beside.wait_send()

        return start, finish, drain

    def slope_x(source, name, hx, a, x):
        up = source[name, rows_of(x + 1), :] if x < NX - 1 else hx[1, a]
        down = source[name, rows_of(x - 1), :] if x > 0 else hx[0, a]
        return up - down

    def slope_y(source, name, hy, a, x):
        if x < NX - 1:
            up = source[name, pl.ds(x * NY + 1, NY), :]
        else:
            up = pltpu.roll(source[name, rows_of(x), :], NY - 1, 0)
        if x > 0:
            down = source[name, pl.ds(x * NY - 1, NY), :]
        else:
            down = pltpu.roll(source[name, rows_of(x), :], 1, 0)
        up = jnp.where(last_row, hy[1, a, pl.ds(x, 1), :], up)
        return up - jnp.where(first_row, hy[0, a, pl.ds(x, 1), :], down)

    def slope_z(source, name, hz, a, x):
        value, beside = source[name, rows_of(x), :], hz[a, rows_of(x), :]
        up = pltpu.roll(jnp.where(first_lane, beside, value), NZ - 1, 1)
        return up - pltpu.roll(jnp.where(last_lane, beside, value), 1, 1)

    def unpack(hz, layers):
        for a in range(3):
            for x in range(NX):
                layers[a, rows_of(x), :] = pltpu.roll(hz[a], NZ - 2 * x, 1) if x else hz[a]

    pack(v, ((0, 1, 2),) * 3, yp1, zp1)
    start1, finish1, drain1 = exchange(
        v.at[:, pl.ds(0, NY), :], v.at[:, pl.ds(ROWS - NY, NY), :], yp1, zp1, hx1, hy1, hz1, hs1_sem, hr1_sem
    )
    start2, finish2, drain2 = exchange(
        xp2.at[0], xp2.at[1], yp2, zp2, hx2, hy2, hz2, hs2_sem, hr2_sem
    )
    start1()

    loads[5].wait()

    def widen(t, carry):
        for a in range(3):
            nf[t, a] = nz[t, a].astype(F32) * (0.1 * SCALE)
        return carry

    lax.fori_loop(0, STEPS, widen, 0)
    loads[6].wait()
    for a in range(3):
        q[a] = q[a] * SCALE

    def chunk(c):
        return pl.ds(c * 128, 128)

    def block_work(order):
        block = block_of(order, 1)
        arrive(order, block, recv1, r1_sem)
        slots = pl.ds(pl.multiple_of(block * BLOCK, BLOCK), BLOCK)
        for s in range(GROUP):
            kst[pl.ds(2 * s, 2), :] = recv1[block * GROUP + s]
        kappa = kst[...] * 0.01
        for k in range(9):
            wide = jnp.broadcast_to(kappa[:, k : k + 1], (BLOCK, 128))
            kb[k] = wide + 1.0 if k % 4 == 0 else wide

        def step(t, state):
            new = []
            for c in range(BEADS // 128):
                q0, q1, q2 = state[3 * c : 3 * c + 3]
                pull = pltpu.reciprocal(
                    jnp.maximum(200.0 - q0 * q0 - (q1 * q1 + q2 * q2), 20.0), approx=True
                )
                for a in range(3):
                    here_q = (q0, q1, q2)[a]
                    other = [b for b in range(3) if b != a]
                    new.append(
                        (kb[4 * a] - pull) * here_q
                        + (kb[3 * a + other[0]] * (q0, q1, q2)[other[0]] + kb[3 * a + other[1]] * (q0, q1, q2)[other[1]])
                        + nf[t, a, slots, chunk(c)]
                    )
            return tuple(new)

        state = tuple(q[a, slots, chunk(c)] for c in range(BEADS // 128) for a in range(3))
        state = lax.fori_loop(0, STEPS, step, state, unroll=UNROLL)
        sums = [None] * 6
        for c in range(BEADS // 128):
            values = state[3 * c : 3 * c + 3]
            q0, q1, q2 = values
            pull = 1.0 / jnp.maximum(200.0 - (q0 * q0 + q1 * q1 + q2 * q2), 20.0)
            for a in range(3):
                q[a, slots, chunk(c)] = values[a] * (1.0 / SCALE)
            pulled = [pull * value for value in values]
            for k, (a, b) in enumerate(PAIRS):
                term = pulled[a] * values[b]
                sums[k] = term if sums[k] is None else sums[k] + term
        lane16 = iota((BLOCK, 128), 1)
        stresses = jnp.zeros((BLOCK, 128), F32)
        for k, (a, b) in enumerate(PAIRS):
            mean = jnp.sum(sums[k], axis=1, keepdims=True) * (30.0 / BEADS)
            stresses = jnp.where(lane16 == k, 0.25 * (mean - (1.0 if a == b else 0.0)), stresses)
        pol[...] = stresses
        for s in range(GROUP):
            send2[block * GROUP + s] = pol[pl.ds(2 * s, 2), :]
        post(order, block, send2, recv2, s2_sem, r2_sem, lambda i: own_row(i).start())

    def stress_work():
        finish1()
        unpack(hz1, layers)
        for x in range(NX):
            grad = {}
            for a in range(3):
                grad[a, 0] = slope_x(v, a, hx1, a, x)
                grad[a, 1] = slope_y(v, a, hy1, a, x)
                grad[a, 2] = slope_z(v, a, layers, a, x)
            half = visc[rows_of(x), :] * 0.5
            for k, (a, b) in enumerate(PAIRS):
                sp[k, rows_of(x), :] = half * (grad[a, b] + grad[b, a])
        for a in range(3):
            xp2[0, a] = sp[SIDE[0][a], rows_of(0), :]
            xp2[1, a] = sp[SIDE[0][a], rows_of(NX - 1), :]
        pack(sp, SIDE, yp2, zp2)
        start2()

    for order in range(NBLOCK):
        if order == STRESS_AT:
            stress_work()
        block_work(order)
    if STRESS_AT == NBLOCK:
        stress_work()

    viscous = jnp.zeros((FLAG, NZ), F32)
    for k, (a, b) in enumerate(PAIRS):
        viscous = jnp.where(lane == k, columns[9] * (columns[3 * a + b] + columns[3 * b + a]), viscous)
    vrow[...] = viscous
    vrow_copy = pltpu.make_async_copy(vrow, vrow_out, out_sem.at[2])
    vrow_copy.start()
    row_col = lax.shift_right_logical(cell_col, 7)
    six = jnp.concatenate([row_col] * 6, axis=0)
    wide0, wide1 = iota((ROWS, ROWS), 0), iota((ROWS, ROWS), 1)
    six_row = jnp.sum(jnp.where(wide0 == wide1, six, 0), axis=0, keepdims=True)
    offset = jnp.where(wide1 < 64, NY, jnp.where(wide1 < 128, 1, 0))
    plus = jnp.where(wide0 == six_row - offset, 1.0, 0.0)
    minus = jnp.where((wide0 == six_row + offset) & (wide1 < 128), 1.0, 0.0)
    amat[...] = (plus - minus).astype(BF16)
    amat_copy = pltpu.make_async_copy(amat, amat_out, out_sem.at[3])
    amat_copy.start()
    conf_copy = pltpu.make_async_copy(q, conf_out, out_sem.at[4])
    conf_copy.start()

    finish2()
    unpack(hz2, layers)
    for x in range(NX):
        for a in range(3):
            total = slope_x(sp, SIDE[0][a], hx2, a, x)
            total = total + slope_y(sp, SIDE[1][a], hy2, a, x)
            total = total + slope_z(sp, SIDE[2][a], layers, a, x)
            vel[a, rows_of(x), :] = v[a, rows_of(x), :] + 0.05 * total

    vel_copy = pltpu.make_async_copy(vel, vel_out, out_sem.at[5])
    vel_copy.start()

    drain1()
    drain2()
    sent(send1, s1_sem)
    sent(send2, s2_sem)
    for copy in (rank_copy, vrow_copy, amat_copy, conf_copy, vel_copy, own_row(me)):
        copy.wait()
    for order in range(NBLOCK):
        arrive(order, block_of(order, 1), recv2, r2_sem)


def finish(
    vel_in, conf_in, back_in, amat_in, vrow_in, rank_in, cell_in, owners_in,
    vel_out, conf_out, fs_out,
    conf, vel, back, amat, vrow, ranks, cellv, owners, prow, stress, in_sem, out_sem,
):
    loads = [
        pltpu.make_async_copy(source, target, in_sem.at[i])
        for i, (source, target) in enumerate(
            (
                (back_in, back), (rank_in, ranks), (owners_in, owners), (cell_in, cellv),
                (vrow_in, vrow), (amat_in, amat), (vel_in, vel), (conf_in, conf),
            )
        )
    ]
    for load in loads:
        load.start()
    for load in loads[:5]:
        load.wait()

    def collect(j, carry):
        prow[pl.ds(j, 1), :] = back[owners[j], pl.ds(ranks[0, j], 1), :]
        return carry

    lax.fori_loop(0, FLAG, collect, 0, unroll=True)
    lane = iota((FLAG, NZ), 1)
    z_col = column(cellv[...]) & (NZ - 1)
    here, above, below = lane == z_col, lane == z_col + 1, lane == z_col - 1
    returned = prow[...]
    flagged = vrow[...] + jnp.where(lane < 6, returned, 0.0)
    pick = (iota((8, NZ), 0) == iota((8, NZ), 1)).astype(F32).astype(BF16)
    turned = None
    for part in pieces(flagged, 3):
        term = lax.dot_general(pick, part, (((1,), (1,)), ((), ())), preferred_element_type=F32)
        turned = term if turned is None else turned + term
    stress[...] = turned[:6, :]
    stress_copy = pltpu.make_async_copy(stress, fs_out, out_sem.at[1])
    stress_copy.start()

    spread = [jnp.broadcast_to(returned[:, k : k + 1] * 0.05, (FLAG, NZ)) for k in range(6)]
    loads[7].wait()
    conf_copy = pltpu.make_async_copy(conf, conf_out, out_sem.at[0])
    conf_copy.start()
    for load in loads[5:7]:
        load.wait()
    for a in range(3):
        parts = []
        parts += pieces(jnp.where(here, spread[SIDE[0][a]], 0.0), 2)
        parts += pieces(jnp.where(here, spread[SIDE[1][a]], 0.0), 2)
        parts += pieces(
            jnp.where(below, spread[SIDE[2][a]], 0.0) - jnp.where(above, spread[SIDE[2][a]], 0.0), 2
        )
        vel[a] = vel[a] + dot(amat[...], jnp.concatenate(parts, axis=0))
        pltpu.make_async_copy(vel.at[a], vel_out.at[a], out_sem.at[2]).start()
    conf_copy.wait()
    stress_copy.wait()
    pltpu.make_async_copy(vel, vel_out, out_sem.at[2]).wait()


def shards(sizes, velocity, viscosity, flag_cell, flag_owner, conformations, increments):
    owner = flag_owner.reshape(FLAG)
    cell_row, owner_row = flag_cell.reshape(1, FLAG), flag_owner.reshape(1, FLAG)
    hbm = pl.BlockSpec(memory_space=pl.ANY)
    vmem = lambda *shape: pltpu.VMEM(shape, F32)
    shape = jax.ShapeDtypeStruct
    scratch = [
        vmem(3, ROWS, NZ), vmem(ROWS, NZ),
        pltpu.SMEM((FLAG,), I32), pltpu.VMEM((1, FLAG), I32), pltpu.VMEM((1, FLAG), I32), pltpu.VMEM((1, FLAG), I32),
        vmem(3, SLOTS, BEADS),
        pltpu.VMEM((STEPS, 3, SLOTS, BEADS), BF16), vmem(STEPS, 3, SLOTS, BEADS),
        vmem(10, FLAG, NZ), vmem(FLAG, NZ), vmem(3, ROWS, NZ),
        vmem(BLOCK, 128), vmem(9, BLOCK, 128), vmem(BLOCK, 128),
        vmem(32, 2, 128), vmem(32, 2, 128), vmem(32, 2, 128),
        vmem(2, 3, NX, NZ), vmem(3, NY, NZ), vmem(2, 3, NY, NZ), vmem(2, 3, NX, NZ), vmem(3, NY, NZ),
        vmem(6, ROWS, NZ),
        vmem(2, 3, NY, NZ), vmem(2, 3, NX, NZ), vmem(3, NY, NZ),
        vmem(2, 3, NY, NZ), vmem(2, 3, NX, NZ), vmem(3, NY, NZ),
        pltpu.VMEM((ROWS, ROWS), BF16), vmem(3, ROWS, NZ),
        pltpu.SemaphoreType.DMA((7,)), pltpu.SemaphoreType.DMA((6,)),
        pltpu.SemaphoreType.DMA, pltpu.SemaphoreType.DMA((NBLOCK,)),
        pltpu.SemaphoreType.DMA, pltpu.SemaphoreType.DMA((NBLOCK,)),
        pltpu.SemaphoreType.DMA((5,)), pltpu.SemaphoreType.DMA((5,)),
        pltpu.SemaphoreType.DMA((5,)), pltpu.SemaphoreType.DMA((5,)),
    ]
    vel, conf = shape((3, ROWS, NZ), F32), shape(conformations.shape, F32)
    held = pl.pallas_call(
        functools.partial(kernel, *sizes),
        out_shape=(
            vel, conf, shape((32, 2, 128), F32), shape((ROWS, ROWS), BF16), shape((FLAG, NZ), F32),
            shape((1, FLAG), I32),
        ),
        in_specs=[hbm] * 7,
        out_specs=(hbm,) * 6,
        scratch_shapes=scratch,
        compiler_params=pltpu.CompilerParams(
            collective_id=0, has_side_effects=True, vmem_limit_bytes=56 * 2**20
        ),
    )(
        velocity.reshape(3, ROWS, NZ), viscosity.reshape(ROWS, NZ),
        flag_cell, cell_row, owner_row, conformations, increments,
    )
    vel, conf, stress = pl.pallas_call(
        finish,
        out_shape=(vel, conf, shape((6, FLAG), F32)),
        in_specs=[hbm] * 8,
        out_specs=(hbm,) * 3,
        scratch_shapes=[
            vmem(3, SLOTS, BEADS), vmem(3, ROWS, NZ), vmem(32, 2, 128), pltpu.VMEM((ROWS, ROWS), BF16), vmem(FLAG, NZ),
            pltpu.SMEM((1, FLAG), I32), pltpu.VMEM((1, FLAG), I32), pltpu.SMEM((FLAG,), I32),
            vmem(FLAG, NZ), vmem(6, FLAG),
            pltpu.SemaphoreType.DMA((8,)), pltpu.SemaphoreType.DMA((3,)),
        ],
        compiler_params=pltpu.CompilerParams(vmem_limit_bytes=56 * 2**20),
    )(*held, cell_row, owner)
    return vel.reshape(velocity.shape), conf, stress


def solution(mesh):
    sizes = (mesh.shape["macro"], mesh.shape["tile"], mesh.shape["micro"])
    in_specs = (
        P(None, "macro", "tile", "micro"),
        P("macro", "tile", "micro"),
        P(("macro", "tile", "micro")),
        P(("macro", "tile", "micro"), None),
        P(None, ("macro", "tile", "micro"), None),
        P(None, None, ("macro", "tile", "micro"), None),
    )
    out_specs = (
        P(None, "macro", "tile", "micro"),
        P(None, ("macro", "tile", "micro"), None),
        P(None, ("macro", "tile", "micro")),
    )
    return jax.shard_map(
        functools.partial(shards, sizes), mesh=mesh, in_specs=in_specs, out_specs=out_specs, check_vma=False
    )
```

```python
import functools
import math

import jax
import jax.numpy as jnp
from jax import lax
from jax.experimental import pallas as pl
from jax.experimental.pallas import tpu as pltpu
from jax.sharding import PartitionSpec as P

MESH = pl.DeviceIdType.MESH
F32, BF16, I32 = jnp.float32, jnp.bfloat16, jnp.int32

PAIRS = ((0, 0), (1, 1), (2, 2), (0, 1), (0, 2), (1, 2))
SIDE = ((0, 3, 4), (3, 1, 5), (4, 5, 2))
SCALE = math.sqrt(200.0 / 30.0)

NX, NY, NZ = 24, 8, 128
ROWS = NX * NY
FLAG = 32
SLOTS = 64
BEADS = 512
STEPS = 16
BLOCK = 16
GROUP = BLOCK // 2
NBLOCK = SLOTS // BLOCK
STRESS_AT = 1
UNROLL = 8
SHIFTS = (0, 2, 1, 3)


def iota(shape, dim):
    return lax.broadcasted_iota(I32, shape, dim)


def pieces(x, count):
    out = []
    for _ in range(count):
        part = x.astype(BF16)
        out.append(part)
        x = x - part.astype(F32)
    return out


def column(row):
    diagonal = iota((FLAG, FLAG), 0) == iota((FLAG, FLAG), 1)
    return jnp.sum(jnp.where(diagonal, row, 0), axis=1, keepdims=True)


def dot(a, b):
    return jnp.dot(a, b, preferred_element_type=F32)


def kernel(
    n_macro, n_tile, n_micro,
    v_in, visc_in, cells_in, cell_in, owner_in, conf_in, noise_in,
    vel_out, conf_out, recv2, amat_out, vrow_out, rank_out,
    v, visc, cells, cellv, ownerv, rankv, q, nz, nf, gat, vrow, vel,
    kst, kb, pol, send1, recv1, send2,
    yp1, zp1, hx1, hy1, hz1, sp, xp2, yp2, zp2, hx2, hy2, hz2, amat, layers,
    in_sem, out_sem, s1_sem, r1_sem, s2_sem, r2_sem, hs1_sem, hr1_sem, hs2_sem, hr2_sem,
):
    macro, tile, micro = lax.axis_index("macro"), lax.axis_index("tile"), lax.axis_index("micro")
    owners_n = n_macro * n_micro
    me = macro * n_micro + micro
    my_block = lax.div(me, GROUP)

    loads = [
        pltpu.make_async_copy(v_in, v, in_sem.at[0]),
        pltpu.make_async_copy(cells_in, cells, in_sem.at[1]),
        pltpu.make_async_copy(cell_in, cellv, in_sem.at[2]),
        pltpu.make_async_copy(owner_in, ownerv, in_sem.at[3]),
        pltpu.make_async_copy(visc_in, visc, in_sem.at[4]),
        pltpu.make_async_copy(noise_in, nz, in_sem.at[5]),
        pltpu.make_async_copy(conf_in, q, in_sem.at[6]),
    ]
    for load in loads:
        load.start()

    barrier = pltpu.get_barrier_semaphore()
    has_up, has_down = tile < n_tile - 1, tile > 0

    def peer_id(peer):
        return (lax.div(peer, n_micro), tile, lax.rem(peer, n_micro))

    def greet(k, carry):
        pl.semaphore_signal(
            barrier, inc=1, device_id=peer_id(lax.rem(me + k, owners_n)), device_id_type=MESH
        )
        return carry

    lax.fori_loop(1, owners_n, greet, 0, unroll=True)

    @pl.when(has_up)
    def _():
        pl.semaphore_signal(barrier, inc=1, device_id=(macro, tile + 1, micro), device_id_type=MESH)

    @pl.when(has_down)
    def _():
        pl.semaphore_signal(barrier, inc=1, device_id=(macro, tile - 1, micro), device_id_type=MESH)

    for load in loads[:5]:
        load.wait()

    def gather(j, carry):
        row = lax.shift_right_logical(cells[j], 7)
        row = jnp.minimum(jnp.maximum(row, NY), ROWS - NY - 1)
        for a in range(3):
            read = lambda offset: v[a, pl.ds(row + offset, 1), :]
            gat[3 * a, pl.ds(j, 1), :] = read(NY) - read(-NY)
            gat[3 * a + 1, pl.ds(j, 1), :] = read(1) - read(-1)
            gat[3 * a + 2, pl.ds(j, 1), :] = read(0)
        gat[9, pl.ds(j, 1), :] = visc[pl.ds(row, 1), :]
        return carry

    lax.fori_loop(0, FLAG, gather, 0, unroll=8)

    square0, square1 = iota((FLAG, FLAG), 0), iota((FLAG, FLAG), 1)
    cell_row, owner_row = cellv[...], ownerv[...]
    cell_col, owner_col = column(cell_row), column(owner_row)
    z_col = cell_col & (NZ - 1)
    lane = iota((FLAG, NZ), 1)
    here, above, below = lane == z_col, lane == z_col + 1, lane == z_col - 1
    rank_row = jnp.sum(
        jnp.where((square0 < square1) & (owner_col == owner_row), 1, 0), axis=0, keepdims=True
    )
    rankv[...] = jnp.minimum(rank_row, 1)
    rank_copy = pltpu.make_async_copy(rankv, rank_out, out_sem.at[0])
    rank_copy.start()

    gathered = jnp.zeros((FLAG, NZ), F32)
    columns = []
    for k in range(10):
        values = gat[k]
        if k < 9 and k % 3 == 2:
            picked = jnp.where(above, values, 0.0) - jnp.where(below, values, 0.0)
        else:
            picked = jnp.where(here, values, 0.0)
        if k < 9:
            picked = picked * 0.5
        columns.append(jnp.sum(picked, axis=1, keepdims=True))
        if k < 9:
            gathered = jnp.where(lane == k, columns[k], gathered)
    position = owner_row * 2 + rank_row
    placing = (iota((SLOTS, FLAG), 0) == position).astype(F32).astype(BF16)
    hi, mid, lo = pieces(gathered, 3)
    outgoing = dot(placing, hi) + (dot(placing, mid) + dot(placing, lo))
    for s in range(owners_n):
        send1[s] = outgoing[2 * s : 2 * s + 2, :]

    @pl.when(has_up & has_down)
    def _():
        pl.semaphore_wait(barrier, owners_n + 1)

    @pl.when(jnp.logical_not(has_up & has_down))
    def _():
        pl.semaphore_wait(barrier, owners_n)

    def block_of(order, sign):
        shift = SHIFTS[order]
        return lax.rem(my_block + sign * shift + NBLOCK, NBLOCK)

    def post(order, block, send, recv, send_sem, recv_sem, own):
        if SHIFTS[order] == 0:
            own(me)
        base = block * GROUP
        turn = me - my_block * GROUP
        for k in range(1 if SHIFTS[order] == 0 else 0, GROUP):
            peer = base + lax.rem(turn + k, GROUP)
            pltpu.make_async_remote_copy(
                src_ref=send.at[peer], dst_ref=recv.at[me],
                send_sem=send_sem, recv_sem=recv_sem.at[my_block],
                device_id=peer_id(peer), device_id_type=MESH,
            ).start()

    def arrive(order, block, recv, recv_sem):
        part = recv.at[pl.ds(0, GROUP - 1 if SHIFTS[order] == 0 else GROUP)]
        pltpu.make_async_copy(part, part, recv_sem.at[block]).wait()

    def sent(send, send_sem):
        part = send.at[pl.ds(0, owners_n - 1)]
        pltpu.make_async_copy(part, part, send_sem).wait()

    def keep_row(i):
        recv1[i] = send1[i]

    def own_row(i):
        return pltpu.make_async_copy(send2.at[i], recv2.at[i], out_sem.at[1])

    for order in range(NBLOCK):
        post(order, block_of(order, -1), send1, recv1, s1_sem, r1_sem, keep_row)

    sub, lanes = iota((NY, NZ), 0), iota((NY, NZ), 1)
    face = lanes == jnp.where(micro == 0, NZ - 1, 0)
    first_lane, last_lane = lanes == 0, lanes == NZ - 1
    first_row, last_row = sub == 0, sub == NY - 1

    def rows_of(x):
        return pl.ds(x * NY, NY)

    def pack(source, names, y_pack, z_pack):
        for a, name in enumerate(names[1]):
            y_pack[0, a] = source[name, pl.ds(0, NX, stride=NY), :]
            y_pack[1, a] = source[name, pl.ds(NY - 1, NX, stride=NY), :]
        for a, name in enumerate(names[2]):
            totals = [None, None, None, None]
            for x in range(NX):
                term = jnp.where(face, source[name, rows_of(x), :], 0.0)
                if x:
                    term = pltpu.roll(term, 2 * x, 1)
                totals[x % 4] = term if totals[x % 4] is None else totals[x % 4] + term
            z_pack[a] = (totals[0] + totals[1]) + (totals[2] + totals[3])

    def exchange(x_low, x_high, y_pack, z_pack, hx, hy, hz, send_sem, recv_sem):
        def remote(i, src, dst, target):
            return pltpu.make_async_remote_copy(
                src_ref=src, dst_ref=dst, send_sem=send_sem.at[i], recv_sem=recv_sem.at[i],
                device_id=target, device_id_type=MESH,
            )

        moves = [
            (macro < n_macro - 1, macro > 0, remote(0, x_high, hx.at[0], (macro + 1, tile, micro)), hx.at[0]),
            (macro > 0, macro < n_macro - 1, remote(1, x_low, hx.at[1], (macro - 1, tile, micro)), hx.at[1]),
            (has_up, has_down, remote(2, y_pack.at[1], hy.at[0], (macro, tile + 1, micro)), hy.at[0]),
            (has_down, has_up, remote(3, y_pack.at[0], hy.at[1], (macro, tile - 1, micro)), hy.at[1]),
        ]
        beside = remote(4, z_pack, hz, (macro, tile, 1 - micro))

        def start():
            for sends, _, copy, _ in moves:
                pl.when(sends)(copy.start)
            beside.start()

        def finish():
            for _, comes, copy, landing in moves:
                pl.when(comes)(copy.wait_recv)

                @pl.when(jnp.logical_not(comes))
                def _():
                    landing[...] = jnp.zeros(landing.shape, F32)

            beside.wait_recv()

        def drain():
            for sends, _, copy, _ in moves:
                pl.when(sends)(copy.wait_send)
            beside.wait_send()

        return start, finish, drain

    def slope_x(source, name, hx, a, x):
        up = source[name, rows_of(x + 1), :] if x < NX - 1 else hx[1, a]
        down = source[name, rows_of(x - 1), :] if x > 0 else hx[0, a]
        return up - down

    def slope_y(source, name, hy, a, x):
        if x < NX - 1:
            up = source[name, pl.ds(x * NY + 1, NY), :]
        else:
            up = pltpu.roll(source[name, rows_of(x), :], NY - 1, 0)
        if x > 0:
            down = source[name, pl.ds(x * NY - 1, NY), :]
        else:
            down = pltpu.roll(source[name, rows_of(x), :], 1, 0)
        up = jnp.where(last_row, hy[1, a, pl.ds(x, 1), :], up)
        return up - jnp.where(first_row, hy[0, a, pl.ds(x, 1), :], down)

    def slope_z(source, name, hz, a, x):
        value, beside = source[name, rows_of(x), :], hz[a, rows_of(x), :]
        up = pltpu.roll(jnp.where(first_lane, beside, value), NZ - 1, 1)
        return up - pltpu.roll(jnp.where(last_lane, beside, value), 1, 1)

    def unpack(hz, layers):
        for a in range(3):
            for x in range(NX):
                layers[a, rows_of(x), :] = pltpu.roll(hz[a], NZ - 2 * x, 1) if x else hz[a]

    pack(v, ((0, 1, 2),) * 3, yp1, zp1)
    start1, finish1, drain1 = exchange(
        v.at[:, pl.ds(0, NY), :], v.at[:, pl.ds(ROWS - NY, NY), :], yp1, zp1, hx1, hy1, hz1, hs1_sem, hr1_sem
    )
    start2, finish2, drain2 = exchange(
        xp2.at[0], xp2.at[1], yp2, zp2, hx2, hy2, hz2, hs2_sem, hr2_sem
    )
    start1()

    loads[5].wait()

    def widen(t, carry):
        for a in range(3):
            nf[t, a] = nz[t, a].astype(F32) * (0.1 * SCALE)
        return carry

    lax.fori_loop(0, STEPS, widen, 0)
    loads[6].wait()
    for a in range(3):
        q[a] = q[a] * SCALE

    def chunk(c):
        return pl.ds(c * 128, 128)

    def block_work(order):
        block = block_of(order, 1)
        arrive(order, block, recv1, r1_sem)
        slots = pl.ds(pl.multiple_of(block * BLOCK, BLOCK), BLOCK)
        for s in range(GROUP):
            kst[pl.ds(2 * s, 2), :] = recv1[block * GROUP + s]
        kappa = kst[...] * 0.01
        for k in range(9):
            wide = jnp.broadcast_to(kappa[:, k : k + 1], (BLOCK, 128))
            kb[k] = wide + 1.0 if k % 4 == 0 else wide

        def step(t, state):
            new = []
            for c in range(BEADS // 128):
                q0, q1, q2 = state[3 * c : 3 * c + 3]
                pull = pltpu.reciprocal(
                    jnp.maximum(200.0 - q0 * q0 - (q1 * q1 + q2 * q2), 20.0), approx=True
                )
                for a in range(3):
                    here_q = (q0, q1, q2)[a]
                    other = [b for b in range(3) if b != a]
                    new.append(
                        (kb[4 * a] - pull) * here_q
                        + (kb[3 * a + other[0]] * (q0, q1, q2)[other[0]] + kb[3 * a + other[1]] * (q0, q1, q2)[other[1]])
                        + nf[t, a, slots, chunk(c)]
                    )
            return tuple(new)

        state = tuple(q[a, slots, chunk(c)] for c in range(BEADS // 128) for a in range(3))
        state = lax.fori_loop(0, STEPS, step, state, unroll=UNROLL)
        sums = [None] * 6
        for c in range(BEADS // 128):
            values = state[3 * c : 3 * c + 3]
            q0, q1, q2 = values
            pull = 1.0 / jnp.maximum(200.0 - (q0 * q0 + q1 * q1 + q2 * q2), 20.0)
            for a in range(3):
                q[a, slots, chunk(c)] = values[a] * (1.0 / SCALE)
            pulled = [pull * value for value in values]
            for k, (a, b) in enumerate(PAIRS):
                term = pulled[a] * values[b]
                sums[k] = term if sums[k] is None else sums[k] + term
        lane16 = iota((BLOCK, 128), 1)
        stresses = jnp.zeros((BLOCK, 128), F32)
        for k, (a, b) in enumerate(PAIRS):
            mean = jnp.sum(sums[k], axis=1, keepdims=True) * (30.0 / BEADS)
            stresses = jnp.where(lane16 == k, 0.25 * (mean - (1.0 if a == b else 0.0)), stresses)
        pol[...] = stresses
        for s in range(GROUP):
            send2[block * GROUP + s] = pol[pl.ds(2 * s, 2), :]
        post(order, block, send2, recv2, s2_sem, r2_sem, lambda i: own_row(i).start())

    def stress_work():
        finish1()
        unpack(hz1, layers)
        for x in range(NX):
            grad = {}
            for a in range(3):
                grad[a, 0] = slope_x(v, a, hx1, a, x)
                grad[a, 1] = slope_y(v, a, hy1, a, x)
                grad[a, 2] = slope_z(v, a, layers, a, x)
            half = visc[rows_of(x), :] * 0.5
            for k, (a, b) in enumerate(PAIRS):
                sp[k, rows_of(x), :] = half * (grad[a, b] + grad[b, a])
        for a in range(3):
            xp2[0, a] = sp[SIDE[0][a], rows_of(0), :]
            xp2[1, a] = sp[SIDE[0][a], rows_of(NX - 1), :]
        pack(sp, SIDE, yp2, zp2)
        start2()

    for order in range(NBLOCK):
        if order == STRESS_AT:
            stress_work()
        block_work(order)
    if STRESS_AT == NBLOCK:
        stress_work()

    viscous = jnp.zeros((FLAG, NZ), F32)
    for k, (a, b) in enumerate(PAIRS):
        viscous = jnp.where(lane == k, columns[9] * (columns[3 * a + b] + columns[3 * b + a]), viscous)
    vrow[...] = viscous
    vrow_copy = pltpu.make_async_copy(vrow, vrow_out, out_sem.at[2])
    vrow_copy.start()
    row_col = lax.shift_right_logical(cell_col, 7)
    six = jnp.concatenate([row_col] * 6, axis=0)
    wide0, wide1 = iota((ROWS, ROWS), 0), iota((ROWS, ROWS), 1)
    six_row = jnp.sum(jnp.where(wide0 == wide1, six, 0), axis=0, keepdims=True)
    offset = jnp.where(wide1 < 64, NY, jnp.where(wide1 < 128, 1, 0))
    plus = jnp.where(wide0 == six_row - offset, 1.0, 0.0)
    minus = jnp.where((wide0 == six_row + offset) & (wide1 < 128), 1.0, 0.0)
    amat[...] = (plus - minus).astype(BF16)
    amat_copy = pltpu.make_async_copy(amat, amat_out, out_sem.at[3])
    amat_copy.start()
    conf_copy = pltpu.make_async_copy(q, conf_out, out_sem.at[4])
    conf_copy.start()

    finish2()
    unpack(hz2, layers)
    for x in range(NX):
        for a in range(3):
            total = slope_x(sp, SIDE[0][a], hx2, a, x)
            total = total + slope_y(sp, SIDE[1][a], hy2, a, x)
            total = total + slope_z(sp, SIDE[2][a], layers, a, x)
            vel[a, rows_of(x), :] = v[a, rows_of(x), :] + 0.05 * total

    vel_copy = pltpu.make_async_copy(vel, vel_out, out_sem.at[5])
    vel_copy.start()

    drain1()
    drain2()
    sent(send1, s1_sem)
    sent(send2, s2_sem)
    for copy in (rank_copy, vrow_copy, amat_copy, conf_copy, vel_copy, own_row(me)):
        copy.wait()
    for order in range(NBLOCK):
        arrive(order, block_of(order, 1), recv2, r2_sem)


def finish(
    vel_in, conf_in, back_in, amat_in, vrow_in, rank_in, cell_in, owners_in,
    vel_out, conf_out, fs_out,
    conf, vel, back, amat, vrow, ranks, cellv, owners, prow, stress, in_sem, out_sem,
):
    loads = [
        pltpu.make_async_copy(source, target, in_sem.at[i])
        for i, (source, target) in enumerate(
            (
                (back_in, back), (rank_in, ranks), (owners_in, owners), (cell_in, cellv),
                (vrow_in, vrow), (amat_in, amat), (vel_in, vel), (conf_in, conf),
            )
        )
    ]
    for load in loads:
        load.start()
    for load in loads[:5]:
        load.wait()

    def collect(j, carry):
        prow[pl.ds(j, 1), :] = back[owners[j], pl.ds(ranks[0, j], 1), :]
        return carry

    lax.fori_loop(0, FLAG, collect, 0, unroll=True)
    lane = iota((FLAG, NZ), 1)
    z_col = column(cellv[...]) & (NZ - 1)
    here, above, below = lane == z_col, lane == z_col + 1, lane == z_col - 1
    returned = prow[...]
    flagged = vrow[...] + jnp.where(lane < 6, returned, 0.0)
    pick = (iota((8, NZ), 0) == iota((8, NZ), 1)).astype(F32).astype(BF16)
    turned = None
    for part in pieces(flagged, 3):
        term = lax.dot_general(pick, part, (((1,), (1,)), ((), ())), preferred_element_type=F32)
        turned = term if turned is None else turned + term
    stress[...] = turned[:6, :]
    stress_copy = pltpu.make_async_copy(stress, fs_out, out_sem.at[1])
    stress_copy.start()

    spread = [jnp.broadcast_to(returned[:, k : k + 1] * 0.05, (FLAG, NZ)) for k in range(6)]
    loads[7].wait()
    conf_copy = pltpu.make_async_copy(conf, conf_out, out_sem.at[0])
    conf_copy.start()
    for load in loads[5:7]:
        load.wait()
    for a in range(3):
        parts = []
        parts += pieces(jnp.where(here, spread[SIDE[0][a]], 0.0), 2)
        parts += pieces(jnp.where(here, spread[SIDE[1][a]], 0.0), 2)
        parts += pieces(
            jnp.where(below, spread[SIDE[2][a]], 0.0) - jnp.where(above, spread[SIDE[2][a]], 0.0), 2
        )
        vel[a] = vel[a] + dot(amat[...], jnp.concatenate(parts, axis=0))
        pltpu.make_async_copy(vel.at[a], vel_out.at[a], out_sem.at[2]).start()
    conf_copy.wait()
    stress_copy.wait()
    pltpu.make_async_copy(vel, vel_out, out_sem.at[2]).wait()


def shards(sizes, velocity, viscosity, flag_cell, flag_owner, conformations, increments):
    owner = flag_owner.reshape(FLAG)
    cell_row, owner_row = flag_cell.reshape(1, FLAG), flag_owner.reshape(1, FLAG)
    hbm = pl.BlockSpec(memory_space=pl.ANY)
    vmem = lambda *shape: pltpu.VMEM(shape, F32)
    shape = jax.ShapeDtypeStruct
    scratch = [
        vmem(3, ROWS, NZ), vmem(ROWS, NZ),
        pltpu.SMEM((FLAG,), I32), pltpu.VMEM((1, FLAG), I32), pltpu.VMEM((1, FLAG), I32), pltpu.VMEM((1, FLAG), I32),
        vmem(3, SLOTS, BEADS),
        pltpu.VMEM((STEPS, 3, SLOTS, BEADS), BF16), vmem(STEPS, 3, SLOTS, BEADS),
        vmem(10, FLAG, NZ), vmem(FLAG, NZ), vmem(3, ROWS, NZ),
        vmem(BLOCK, 128), vmem(9, BLOCK, 128), vmem(BLOCK, 128),
        vmem(32, 2, 128), vmem(32, 2, 128), vmem(32, 2, 128),
        vmem(2, 3, NX, NZ), vmem(3, NY, NZ), vmem(2, 3, NY, NZ), vmem(2, 3, NX, NZ), vmem(3, NY, NZ),
        vmem(6, ROWS, NZ),
        vmem(2, 3, NY, NZ), vmem(2, 3, NX, NZ), vmem(3, NY, NZ),
        vmem(2, 3, NY, NZ), vmem(2, 3, NX, NZ), vmem(3, NY, NZ),
        pltpu.VMEM((ROWS, ROWS), BF16), vmem(3, ROWS, NZ),
        pltpu.SemaphoreType.DMA((7,)), pltpu.SemaphoreType.DMA((6,)),
        pltpu.SemaphoreType.DMA, pltpu.SemaphoreType.DMA((NBLOCK,)),
        pltpu.SemaphoreType.DMA, pltpu.SemaphoreType.DMA((NBLOCK,)),
        pltpu.SemaphoreType.DMA((5,)), pltpu.SemaphoreType.DMA((5,)),
        pltpu.SemaphoreType.DMA((5,)), pltpu.SemaphoreType.DMA((5,)),
    ]
    vel, conf = shape((3, ROWS, NZ), F32), shape(conformations.shape, F32)
    held = pl.pallas_call(
        functools.partial(kernel, *sizes),
        out_shape=(
            vel, conf, shape((32, 2, 128), F32), shape((ROWS, ROWS), BF16), shape((FLAG, NZ), F32),
            shape((1, FLAG), I32),
        ),
        in_specs=[hbm] * 7,
        out_specs=(hbm,) * 6,
        scratch_shapes=scratch,
        compiler_params=pltpu.CompilerParams(
            collective_id=0, has_side_effects=True, vmem_limit_bytes=56 * 2**20
        ),
    )(
        velocity.reshape(3, ROWS, NZ), viscosity.reshape(ROWS, NZ),
        flag_cell, cell_row, owner_row, conformations, increments,
    )
    vel, conf, stress = pl.pallas_call(
        finish,
        out_shape=(vel, conf, shape((6, FLAG), F32)),
        in_specs=[hbm] * 8,
        out_specs=(hbm,) * 3,
        scratch_shapes=[
            vmem(3, SLOTS, BEADS), vmem(3, ROWS, NZ), vmem(32, 2, 128), pltpu.VMEM((ROWS, ROWS), BF16), vmem(FLAG, NZ),
            pltpu.SMEM((1, FLAG), I32), pltpu.VMEM((1, FLAG), I32), pltpu.SMEM((FLAG,), I32),
            vmem(FLAG, NZ), vmem(6, FLAG),
            pltpu.SemaphoreType.DMA((8,)), pltpu.SemaphoreType.DMA((3,)),
        ],
        compiler_params=pltpu.CompilerParams(vmem_limit_bytes=56 * 2**20),
    )(*held, cell_row, owner)
    return vel.reshape(velocity.shape), conf, stress


def solution(mesh):
    sizes = (mesh.shape["macro"], mesh.shape["tile"], mesh.shape["micro"])
    in_specs = (
        P(None, "macro", "tile", "micro"),
        P("macro", "tile", "micro"),
        P(("macro", "tile", "micro")),
        P(("macro", "tile", "micro"), None),
        P(None, ("macro", "tile", "micro"), None),
        P(None, None, ("macro", "tile", "micro"), None),
    )
    out_specs = (
        P(None, "macro", "tile", "micro"),
        P(None, ("macro", "tile", "micro"), None),
        P(None, ("macro", "tile", "micro")),
    )
    return jax.shard_map(
        functools.partial(shards, sizes), mesh=mesh, in_specs=in_specs, out_specs=out_specs, check_vma=False
    )
```

```python
import functools
import math

import jax
import jax.numpy as jnp
from jax import lax
from jax.experimental import pallas as pl
from jax.experimental.pallas import tpu as pltpu
from jax.sharding import PartitionSpec as P

MESH = pl.DeviceIdType.MESH
F32, BF16, I32 = jnp.float32, jnp.bfloat16, jnp.int32

PAIRS = ((0, 0), (1, 1), (2, 2), (0, 1), (0, 2), (1, 2))
SIDE = ((0, 3, 4), (3, 1, 5), (4, 5, 2))
SCALE = math.sqrt(200.0 / 30.0)

NX, NY, NZ = 24, 8, 128
ROWS = NX * NY
FLAG = 32
SLOTS = 64
BEADS = 512
STEPS = 16
BLOCK = 16
GROUP = BLOCK // 2
NBLOCK = SLOTS // BLOCK
STRESS_AT = 2
UNROLL = 8
SHIFTS = (1, 2, 3, 0)


def iota(shape, dim):
    return lax.broadcasted_iota(I32, shape, dim)


def pieces(x, count):
    out = []
    for _ in range(count):
        part = x.astype(BF16)
        out.append(part)
        x = x - part.astype(F32)
    return out


def column(row):
    diagonal = iota((FLAG, FLAG), 0) == iota((FLAG, FLAG), 1)
    return jnp.sum(jnp.where(diagonal, row, 0), axis=1, keepdims=True)


def dot(a, b):
    return jnp.dot(a, b, preferred_element_type=F32)


def kernel(
    n_macro, n_tile, n_micro,
    v_in, visc_in, cells_in, cell_in, owner_in, conf_in, noise_in,
    vel_out, conf_out, recv2, amat_out, vrow_out, rank_out,
    v, visc, cells, cellv, ownerv, rankv, q, nz, nf, gat, vrow, vel,
    kst, kb, pol, send1, recv1, send2,
    yp1, zp1, hx1, hy1, hz1, sp, xp2, yp2, zp2, hx2, hy2, hz2, amat, layers,
    in_sem, out_sem, s1_sem, r1_sem, s2_sem, r2_sem, hs1_sem, hr1_sem, hs2_sem, hr2_sem,
):
    macro, tile, micro = lax.axis_index("macro"), lax.axis_index("tile"), lax.axis_index("micro")
    owners_n = n_macro * n_micro
    me = macro * n_micro + micro
    my_block = lax.div(me, GROUP)

    loads = [
        pltpu.make_async_copy(v_in, v, in_sem.at[0]),
        pltpu.make_async_copy(cells_in, cells, in_sem.at[1]),
        pltpu.make_async_copy(cell_in, cellv, in_sem.at[2]),
        pltpu.make_async_copy(owner_in, ownerv, in_sem.at[3]),
        pltpu.make_async_copy(visc_in, visc, in_sem.at[4]),
        pltpu.make_async_copy(noise_in, nz, in_sem.at[5]),
        pltpu.make_async_copy(conf_in, q, in_sem.at[6]),
    ]
    for load in loads:
        load.start()

    barrier = pltpu.get_barrier_semaphore()
    has_up, has_down = tile < n_tile - 1, tile > 0

    def peer_id(peer):
        return (lax.div(peer, n_micro), tile, lax.rem(peer, n_micro))

    def greet(k, carry):
        pl.semaphore_signal(
            barrier, inc=1, device_id=peer_id(lax.rem(me + k, owners_n)), device_id_type=MESH
        )
        return carry

    lax.fori_loop(1, owners_n, greet, 0, unroll=True)

    @pl.when(has_up)
    def _():
        pl.semaphore_signal(barrier, inc=1, device_id=(macro, tile + 1, micro), device_id_type=MESH)

    @pl.when(has_down)
    def _():
        pl.semaphore_signal(barrier, inc=1, device_id=(macro, tile - 1, micro), device_id_type=MESH)

    for load in loads[:5]:
        load.wait()

    def gather(j, carry):
        row = lax.shift_right_logical(cells[j], 7)
        row = jnp.minimum(jnp.maximum(row, NY), ROWS - NY - 1)
        for a in range(3):
            read = lambda offset: v[a, pl.ds(row + offset, 1), :]
            gat[3 * a, pl.ds(j, 1), :] = read(NY) - read(-NY)
            gat[3 * a + 1, pl.ds(j, 1), :] = read(1) - read(-1)
            gat[3 * a + 2, pl.ds(j, 1), :] = read(0)
        gat[9, pl.ds(j, 1), :] = visc[pl.ds(row, 1), :]
        return carry

    lax.fori_loop(0, FLAG, gather, 0, unroll=8)

    square0, square1 = iota((FLAG, FLAG), 0), iota((FLAG, FLAG), 1)
    cell_row, owner_row = cellv[...], ownerv[...]
    cell_col, owner_col = column(cell_row), column(owner_row)
    z_col = cell_col & (NZ - 1)
    lane = iota((FLAG, NZ), 1)
    here, above, below = lane == z_col, lane == z_col + 1, lane == z_col - 1
    rank_row = jnp.sum(
        jnp.where((square0 < square1) & (owner_col == owner_row), 1, 0), axis=0, keepdims=True
    )
    rankv[...] = jnp.minimum(rank_row, 1)
    rank_copy = pltpu.make_async_copy(rankv, rank_out, out_sem.at[0])
    rank_copy.start()

    gathered = jnp.zeros((FLAG, NZ), F32)
    columns = []
    for k in range(10):
        values = gat[k]
        if k < 9 and k % 3 == 2:
            picked = jnp.where(above, values, 0.0) - jnp.where(below, values, 0.0)
        else:
            picked = jnp.where(here, values, 0.0)
        if k < 9:
            picked = picked * 0.5
        columns.append(jnp.sum(picked, axis=1, keepdims=True))
        if k < 9:
            gathered = jnp.where(lane == k, columns[k], gathered)
    position = owner_row * 2 + rank_row
    placing = (iota((SLOTS, FLAG), 0) == position).astype(F32).astype(BF16)
    hi, mid, lo = pieces(gathered, 3)
    outgoing = dot(placing, hi) + (dot(placing, mid) + dot(placing, lo))
    for s in range(owners_n):
        send1[s] = outgoing[2 * s : 2 * s + 2, :]

    @pl.when(has_up & has_down)
    def _():
        pl.semaphore_wait(barrier, owners_n + 1)

    @pl.when(jnp.logical_not(has_up & has_down))
    def _():
        pl.semaphore_wait(barrier, owners_n)

    def block_of(order, sign):
        shift = SHIFTS[order]
        return lax.rem(my_block + sign * shift + NBLOCK, NBLOCK)

    def post(order, block, send, recv, send_sem, recv_sem, own):
        if SHIFTS[order] == 0:
            own(me)
        base = block * GROUP
        turn = me - my_block * GROUP
        for k in range(1 if SHIFTS[order] == 0 else 0, GROUP):
            peer = base + lax.rem(turn + k, GROUP)
            pltpu.make_async_remote_copy(
                src_ref=send.at[peer], dst_ref=recv.at[me],
                send_sem=send_sem, recv_sem=recv_sem.at[my_block],
                device_id=peer_id(peer), device_id_type=MESH,
            ).start()

    def arrive(order, block, recv, recv_sem):
        part = recv.at[pl.ds(0, GROUP - 1 if SHIFTS[order] == 0 else GROUP)]
        pltpu.make_async_copy(part, part, recv_sem.at[block]).wait()

    def sent(send, send_sem):
        part = send.at[pl.ds(0, owners_n - 1)]
        pltpu.make_async_copy(part, part, send_sem).wait()

    def keep_row(i):
        recv1[i] = send1[i]

    def own_row(i):
        return pltpu.make_async_copy(send2.at[i], recv2.at[i], out_sem.at[1])

    for order in range(NBLOCK):
        post(order, block_of(order, -1), send1, recv1, s1_sem, r1_sem, keep_row)

    sub, lanes = iota((NY, NZ), 0), iota((NY, NZ), 1)
    face = lanes == jnp.where(micro == 0, NZ - 1, 0)
    first_lane, last_lane = lanes == 0, lanes == NZ - 1
    first_row, last_row = sub == 0, sub == NY - 1

    def rows_of(x):
        return pl.ds(x * NY, NY)

    def pack(source, names, y_pack, z_pack):
        for a, name in enumerate(names[1]):
            y_pack[0, a] = source[name, pl.ds(0, NX, stride=NY), :]
            y_pack[1, a] = source[name, pl.ds(NY - 1, NX, stride=NY), :]
        for a, name in enumerate(names[2]):
            totals = [None, None, None, None]
            for x in range(NX):
                term = jnp.where(face, source[name, rows_of(x), :], 0.0)
                if x:
                    term = pltpu.roll(term, 2 * x, 1)
                totals[x % 4] = term if totals[x % 4] is None else totals[x % 4] + term
            z_pack[a] = (totals[0] + totals[1]) + (totals[2] + totals[3])

    def exchange(x_low, x_high, y_pack, z_pack, hx, hy, hz, send_sem, recv_sem):
        def remote(i, src, dst, target):
            return pltpu.make_async_remote_copy(
                src_ref=src, dst_ref=dst, send_sem=send_sem.at[i], recv_sem=recv_sem.at[i],
                device_id=target, device_id_type=MESH,
            )

        moves = [
            (macro < n_macro - 1, macro > 0, remote(0, x_high, hx.at[0], (macro + 1, tile, micro)), hx.at[0]),
            (macro > 0, macro < n_macro - 1, remote(1, x_low, hx.at[1], (macro - 1, tile, micro)), hx.at[1]),
            (has_up, has_down, remote(2, y_pack.at[1], hy.at[0], (macro, tile + 1, micro)), hy.at[0]),
            (has_down, has_up, remote(3, y_pack.at[0], hy.at[1], (macro, tile - 1, micro)), hy.at[1]),
        ]
        beside = remote(4, z_pack, hz, (macro, tile, 1 - micro))

        def start():
            for sends, _, copy, _ in moves:
                pl.when(sends)(copy.start)
            beside.start()

        def finish():
            for _, comes, copy, landing in moves:
                pl.when(comes)(copy.wait_recv)

                @pl.when(jnp.logical_not(comes))
                def _():
                    landing[...] = jnp.zeros(landing.shape, F32)

            beside.wait_recv()

        def drain():
            for sends, _, copy, _ in moves:
                pl.when(sends)(copy.wait_send)
            beside.wait_send()

        return start, finish, drain

    def slope_x(source, name, hx, a, x):
        up = source[name, rows_of(x + 1), :] if x < NX - 1 else hx[1, a]
        down = source[name, rows_of(x - 1), :] if x > 0 else hx[0, a]
        return up - down

    def slope_y(source, name, hy, a, x):
        if x < NX - 1:
            up = source[name, pl.ds(x * NY + 1, NY), :]
        else:
            up = pltpu.roll(source[name, rows_of(x), :], NY - 1, 0)
        if x > 0:
            down = source[name, pl.ds(x * NY - 1, NY), :]
        else:
            down = pltpu.roll(source[name, rows_of(x), :], 1, 0)
        up = jnp.where(last_row, hy[1, a, pl.ds(x, 1), :], up)
        return up - jnp.where(first_row, hy[0, a, pl.ds(x, 1), :], down)

    def slope_z(source, name, hz, a, x):
        value, beside = source[name, rows_of(x), :], hz[a, rows_of(x), :]
        up = pltpu.roll(jnp.where(first_lane, beside, value), NZ - 1, 1)
        return up - pltpu.roll(jnp.where(last_lane, beside, value), 1, 1)

    def unpack(hz, layers):
        for a in range(3):
            for x in range(NX):
                layers[a, rows_of(x), :] = pltpu.roll(hz[a], NZ - 2 * x, 1) if x else hz[a]

    pack(v, ((0, 1, 2),) * 3, yp1, zp1)
    start1, finish1, drain1 = exchange(
        v.at[:, pl.ds(0, NY), :], v.at[:, pl.ds(ROWS - NY, NY), :], yp1, zp1, hx1, hy1, hz1, hs1_sem, hr1_sem
    )
    start2, finish2, drain2 = exchange(
        xp2.at[0], xp2.at[1], yp2, zp2, hx2, hy2, hz2, hs2_sem, hr2_sem
    )
    start1()

    loads[5].wait()

    def widen(t, carry):
        for a in range(3):
            nf[t, a] = nz[t, a].astype(F32) * (0.1 * SCALE)
        return carry

    lax.fori_loop(0, STEPS, widen, 0)
    loads[6].wait()
    for a in range(3):
        q[a] = q[a] * SCALE

    def chunk(c):
        return pl.ds(c * 128, 128)

    def block_work(order):
        block = block_of(order, 1)
        arrive(order, block, recv1, r1_sem)
        slots = pl.ds(pl.multiple_of(block * BLOCK, BLOCK), BLOCK)
        for s in range(GROUP):
            kst[pl.ds(2 * s, 2), :] = recv1[block * GROUP + s]
        kappa = kst[...] * 0.01
        for k in range(9):
            wide = jnp.broadcast_to(kappa[:, k : k + 1], (BLOCK, 128))
            kb[k] = wide + 1.0 if k % 4 == 0 else wide

        def step(t, state):
            new = []
            for c in range(BEADS // 128):
                q0, q1, q2 = state[3 * c : 3 * c + 3]
                pull = pltpu.reciprocal(
                    jnp.maximum(200.0 - q0 * q0 - (q1 * q1 + q2 * q2), 20.0), approx=True
                )
                for a in range(3):
                    here_q = (q0, q1, q2)[a]
                    other = [b for b in range(3) if b != a]
                    new.append(
                        (kb[4 * a] - pull) * here_q
                        + (kb[3 * a + other[0]] * (q0, q1, q2)[other[0]] + kb[3 * a + other[1]] * (q0, q1, q2)[other[1]])
                        + nf[t, a, slots, chunk(c)]
                    )
            return tuple(new)

        state = tuple(q[a, slots, chunk(c)] for c in range(BEADS // 128) for a in range(3))
        state = lax.fori_loop(0, STEPS, step, state, unroll=UNROLL)
        sums = [None] * 6
        for c in range(BEADS // 128):
            values = state[3 * c : 3 * c + 3]
            q0, q1, q2 = values
            pull = 1.0 / jnp.maximum(200.0 - (q0 * q0 + q1 * q1 + q2 * q2), 20.0)
            for a in range(3):
                q[a, slots, chunk(c)] = values[a] * (1.0 / SCALE)
            pulled = [pull * value for value in values]
            for k, (a, b) in enumerate(PAIRS):
                term = pulled[a] * values[b]
                sums[k] = term if sums[k] is None else sums[k] + term
        lane16 = iota((BLOCK, 128), 1)
        stresses = jnp.zeros((BLOCK, 128), F32)
        for k, (a, b) in enumerate(PAIRS):
            mean = jnp.sum(sums[k], axis=1, keepdims=True) * (30.0 / BEADS)
            stresses = jnp.where(lane16 == k, 0.25 * (mean - (1.0 if a == b else 0.0)), stresses)
        pol[...] = stresses
        for s in range(GROUP):
            send2[block * GROUP + s] = pol[pl.ds(2 * s, 2), :]
        post(order, block, send2, recv2, s2_sem, r2_sem, lambda i: own_row(i).start())

    def stress_work():
        finish1()
        unpack(hz1, layers)
        for x in range(NX):
            grad = {}
            for a in range(3):
                grad[a, 0] = slope_x(v, a, hx1, a, x)
                grad[a, 1] = slope_y(v, a, hy1, a, x)
                grad[a, 2] = slope_z(v, a, layers, a, x)
            half = visc[rows_of(x), :] * 0.5
            for k, (a, b) in enumerate(PAIRS):
                sp[k, rows_of(x), :] = half * (grad[a, b] + grad[b, a])
        for a in range(3):
            xp2[0, a] = sp[SIDE[0][a], rows_of(0), :]
            xp2[1, a] = sp[SIDE[0][a], rows_of(NX - 1), :]
        pack(sp, SIDE, yp2, zp2)
        start2()

    for order in range(NBLOCK):
        if order == STRESS_AT:
            stress_work()
        block_work(order)
    if STRESS_AT == NBLOCK:
        stress_work()

    viscous = jnp.zeros((FLAG, NZ), F32)
    for k, (a, b) in enumerate(PAIRS):
        viscous = jnp.where(lane == k, columns[9] * (columns[3 * a + b] + columns[3 * b + a]), viscous)
    vrow[...] = viscous
    vrow_copy = pltpu.make_async_copy(vrow, vrow_out, out_sem.at[2])
    vrow_copy.start()
    row_col = lax.shift_right_logical(cell_col, 7)
    six = jnp.concatenate([row_col] * 6, axis=0)
    wide0, wide1 = iota((ROWS, ROWS), 0), iota((ROWS, ROWS), 1)
    six_row = jnp.sum(jnp.where(wide0 == wide1, six, 0), axis=0, keepdims=True)
    offset = jnp.where(wide1 < 64, NY, jnp.where(wide1 < 128, 1, 0))
    plus = jnp.where(wide0 == six_row - offset, 1.0, 0.0)
    minus = jnp.where((wide0 == six_row + offset) & (wide1 < 128), 1.0, 0.0)
    amat[...] = (plus - minus).astype(BF16)
    amat_copy = pltpu.make_async_copy(amat, amat_out, out_sem.at[3])
    amat_copy.start()
    conf_copy = pltpu.make_async_copy(q, conf_out, out_sem.at[4])
    conf_copy.start()

    finish2()
    unpack(hz2, layers)
    for x in range(NX):
        for a in range(3):
            total = slope_x(sp, SIDE[0][a], hx2, a, x)
            total = total + slope_y(sp, SIDE[1][a], hy2, a, x)
            total = total + slope_z(sp, SIDE[2][a], layers, a, x)
            vel[a, rows_of(x), :] = v[a, rows_of(x), :] + 0.05 * total

    vel_copy = pltpu.make_async_copy(vel, vel_out, out_sem.at[5])
    vel_copy.start()

    drain1()
    drain2()
    sent(send1, s1_sem)
    sent(send2, s2_sem)
    for copy in (rank_copy, vrow_copy, amat_copy, conf_copy, vel_copy, own_row(me)):
        copy.wait()
    for order in range(NBLOCK):
        arrive(order, block_of(order, 1), recv2, r2_sem)


def finish(
    vel_in, conf_in, back_in, amat_in, vrow_in, rank_in, cell_in, owners_in,
    vel_out, conf_out, fs_out,
    conf, vel, back, amat, vrow, ranks, cellv, owners, prow, stress, in_sem, out_sem,
):
    loads = [
        pltpu.make_async_copy(source, target, in_sem.at[i])
        for i, (source, target) in enumerate(
            (
                (back_in, back), (rank_in, ranks), (owners_in, owners), (cell_in, cellv),
                (vrow_in, vrow), (amat_in, amat), (vel_in, vel), (conf_in, conf),
            )
        )
    ]
    for load in loads:
        load.start()
    for load in loads[:5]:
        load.wait()

    def collect(j, carry):
        prow[pl.ds(j, 1), :] = back[owners[j], pl.ds(ranks[0, j], 1), :]
        return carry

    lax.fori_loop(0, FLAG, collect, 0, unroll=True)
    lane = iota((FLAG, NZ), 1)
    z_col = column(cellv[...]) & (NZ - 1)
    here, above, below = lane == z_col, lane == z_col + 1, lane == z_col - 1
    returned = prow[...]
    flagged = vrow[...] + jnp.where(lane < 6, returned, 0.0)
    pick = (iota((8, NZ), 0) == iota((8, NZ), 1)).astype(F32).astype(BF16)
    turned = None
    for part in pieces(flagged, 3):
        term = lax.dot_general(pick, part, (((1,), (1,)), ((), ())), preferred_element_type=F32)
        turned = term if turned is None else turned + term
    stress[...] = turned[:6, :]
    stress_copy = pltpu.make_async_copy(stress, fs_out, out_sem.at[1])
    stress_copy.start()

    spread = [jnp.broadcast_to(returned[:, k : k + 1] * 0.05, (FLAG, NZ)) for k in range(6)]
    loads[7].wait()
    conf_copy = pltpu.make_async_copy(conf, conf_out, out_sem.at[0])
    conf_copy.start()
    for load in loads[5:7]:
        load.wait()
    for a in range(3):
        parts = []
        parts += pieces(jnp.where(here, spread[SIDE[0][a]], 0.0), 2)
        parts += pieces(jnp.where(here, spread[SIDE[1][a]], 0.0), 2)
        parts += pieces(
            jnp.where(below, spread[SIDE[2][a]], 0.0) - jnp.where(above, spread[SIDE[2][a]], 0.0), 2
        )
        vel[a] = vel[a] + dot(amat[...], jnp.concatenate(parts, axis=0))
        pltpu.make_async_copy(vel.at[a], vel_out.at[a], out_sem.at[2]).start()
    conf_copy.wait()
    stress_copy.wait()
    pltpu.make_async_copy(vel, vel_out, out_sem.at[2]).wait()


def shards(sizes, velocity, viscosity, flag_cell, flag_owner, conformations, increments):
    owner = flag_owner.reshape(FLAG)
    cell_row, owner_row = flag_cell.reshape(1, FLAG), flag_owner.reshape(1, FLAG)
    hbm = pl.BlockSpec(memory_space=pl.ANY)
    vmem = lambda *shape: pltpu.VMEM(shape, F32)
    shape = jax.ShapeDtypeStruct
    scratch = [
        vmem(3, ROWS, NZ), vmem(ROWS, NZ),
        pltpu.SMEM((FLAG,), I32), pltpu.VMEM((1, FLAG), I32), pltpu.VMEM((1, FLAG), I32), pltpu.VMEM((1, FLAG), I32),
        vmem(3, SLOTS, BEADS),
        pltpu.VMEM((STEPS, 3, SLOTS, BEADS), BF16), vmem(STEPS, 3, SLOTS, BEADS),
        vmem(10, FLAG, NZ), vmem(FLAG, NZ), vmem(3, ROWS, NZ),
        vmem(BLOCK, 128), vmem(9, BLOCK, 128), vmem(BLOCK, 128),
        vmem(32, 2, 128), vmem(32, 2, 128), vmem(32, 2, 128),
        vmem(2, 3, NX, NZ), vmem(3, NY, NZ), vmem(2, 3, NY, NZ), vmem(2, 3, NX, NZ), vmem(3, NY, NZ),
        vmem(6, ROWS, NZ),
        vmem(2, 3, NY, NZ), vmem(2, 3, NX, NZ), vmem(3, NY, NZ),
        vmem(2, 3, NY, NZ), vmem(2, 3, NX, NZ), vmem(3, NY, NZ),
        pltpu.VMEM((ROWS, ROWS), BF16), vmem(3, ROWS, NZ),
        pltpu.SemaphoreType.DMA((7,)), pltpu.SemaphoreType.DMA((6,)),
        pltpu.SemaphoreType.DMA, pltpu.SemaphoreType.DMA((NBLOCK,)),
        pltpu.SemaphoreType.DMA, pltpu.SemaphoreType.DMA((NBLOCK,)),
        pltpu.SemaphoreType.DMA((5,)), pltpu.SemaphoreType.DMA((5,)),
        pltpu.SemaphoreType.DMA((5,)), pltpu.SemaphoreType.DMA((5,)),
    ]
    vel, conf = shape((3, ROWS, NZ), F32), shape(conformations.shape, F32)
    held = pl.pallas_call(
        functools.partial(kernel, *sizes),
        out_shape=(
            vel, conf, shape((32, 2, 128), F32), shape((ROWS, ROWS), BF16), shape((FLAG, NZ), F32),
            shape((1, FLAG), I32),
        ),
        in_specs=[hbm] * 7,
        out_specs=(hbm,) * 6,
        scratch_shapes=scratch,
        compiler_params=pltpu.CompilerParams(
            collective_id=0, has_side_effects=True, vmem_limit_bytes=56 * 2**20
        ),
    )(
        velocity.reshape(3, ROWS, NZ), viscosity.reshape(ROWS, NZ),
        flag_cell, cell_row, owner_row, conformations, increments,
    )
    vel, conf, stress = pl.pallas_call(
        finish,
        out_shape=(vel, conf, shape((6, FLAG), F32)),
        in_specs=[hbm] * 8,
        out_specs=(hbm,) * 3,
        scratch_shapes=[
            vmem(3, SLOTS, BEADS), vmem(3, ROWS, NZ), vmem(32, 2, 128), pltpu.VMEM((ROWS, ROWS), BF16), vmem(FLAG, NZ),
            pltpu.SMEM((1, FLAG), I32), pltpu.VMEM((1, FLAG), I32), pltpu.SMEM((FLAG,), I32),
            vmem(FLAG, NZ), vmem(6, FLAG),
            pltpu.SemaphoreType.DMA((8,)), pltpu.SemaphoreType.DMA((3,)),
        ],
        compiler_params=pltpu.CompilerParams(vmem_limit_bytes=56 * 2**20),
    )(*held, cell_row, owner)
    return vel.reshape(velocity.shape), conf, stress


def solution(mesh):
    sizes = (mesh.shape["macro"], mesh.shape["tile"], mesh.shape["micro"])
    in_specs = (
        P(None, "macro", "tile", "micro"),
        P("macro", "tile", "micro"),
        P(("macro", "tile", "micro")),
        P(("macro", "tile", "micro"), None),
        P(None, ("macro", "tile", "micro"), None),
        P(None, None, ("macro", "tile", "micro"), None),
    )
    out_specs = (
        P(None, "macro", "tile", "micro"),
        P(None, ("macro", "tile", "micro"), None),
        P(None, ("macro", "tile", "micro")),
    )
    return jax.shard_map(
        functools.partial(shards, sizes), mesh=mesh, in_specs=in_specs, out_specs=out_specs, check_vma=False
    )
```

```python
import functools
import math

import jax
import jax.numpy as jnp
from jax import lax
from jax.experimental import pallas as pl
from jax.experimental.pallas import tpu as pltpu
from jax.sharding import PartitionSpec as P

MESH = pl.DeviceIdType.MESH
F32, BF16, I32 = jnp.float32, jnp.bfloat16, jnp.int32

PAIRS = ((0, 0), (1, 1), (2, 2), (0, 1), (0, 2), (1, 2))
SIDE = ((0, 3, 4), (3, 1, 5), (4, 5, 2))
SCALE = math.sqrt(200.0 / 30.0)

NX, NY, NZ = 24, 8, 128
ROWS = NX * NY
FLAG = 32
SLOTS = 64
BEADS = 512
STEPS = 16
BLOCK = 16
GROUP = BLOCK // 2
NBLOCK = SLOTS // BLOCK
STRESS_AT = 1
UNROLL = 8
SHIFTS = (0, 2, 1, 3)


def iota(shape, dim):
    return lax.broadcasted_iota(I32, shape, dim)


def pieces(x, count):
    out = []
    for _ in range(count):
        part = x.astype(BF16)
        out.append(part)
        x = x - part.astype(F32)
    return out


def column(row):
    diagonal = iota((FLAG, FLAG), 0) == iota((FLAG, FLAG), 1)
    return jnp.sum(jnp.where(diagonal, row, 0), axis=1, keepdims=True)


def dot(a, b):
    return jnp.dot(a, b, preferred_element_type=F32)


def kernel(
    n_macro, n_tile, n_micro,
    v_in, visc_in, cells_in, cell_in, owner_in, conf_in, noise_in,
    vel_out, conf_out, recv2, amat_out, vrow_out, rank_out,
    v, visc, cells, cellv, ownerv, rankv, q, nz, nf, gat, vrow, vel,
    kst, kb, pol, send1, recv1, send2,
    yp1, zp1, hx1, hy1, hz1, sp, xp2, yp2, zp2, hx2, hy2, hz2, amat, layers,
    in_sem, out_sem, s1_sem, r1_sem, s2_sem, r2_sem, hs1_sem, hr1_sem, hs2_sem, hr2_sem,
):
    macro, tile, micro = lax.axis_index("macro"), lax.axis_index("tile"), lax.axis_index("micro")
    owners_n = n_macro * n_micro
    me = macro * n_micro + micro
    my_block = lax.div(me, GROUP)

    loads = [
        pltpu.make_async_copy(v_in, v, in_sem.at[0]),
        pltpu.make_async_copy(cells_in, cells, in_sem.at[1]),
        pltpu.make_async_copy(cell_in, cellv, in_sem.at[2]),
        pltpu.make_async_copy(owner_in, ownerv, in_sem.at[3]),
        pltpu.make_async_copy(visc_in, visc, in_sem.at[4]),
        pltpu.make_async_copy(noise_in, nz, in_sem.at[5]),
        pltpu.make_async_copy(conf_in, q, in_sem.at[6]),
    ]
    for load in loads:
        load.start()

    barrier = pltpu.get_barrier_semaphore()
    has_up, has_down = tile < n_tile - 1, tile > 0

    def peer_id(peer):
        return (lax.div(peer, n_micro), tile, lax.rem(peer, n_micro))

    def greet(k, carry):
        pl.semaphore_signal(
            barrier, inc=1, device_id=peer_id(lax.rem(me + k, owners_n)), device_id_type=MESH
        )
        return carry

    lax.fori_loop(1, owners_n, greet, 0, unroll=True)

    @pl.when(has_up)
    def _():
        pl.semaphore_signal(barrier, inc=1, device_id=(macro, tile + 1, micro), device_id_type=MESH)

    @pl.when(has_down)
    def _():
        pl.semaphore_signal(barrier, inc=1, device_id=(macro, tile - 1, micro), device_id_type=MESH)

    for load in loads[:5]:
        load.wait()

    def gather(j, carry):
        row = lax.shift_right_logical(cells[j], 7)
        row = jnp.minimum(jnp.maximum(row, NY), ROWS - NY - 1)
        for a in range(3):
            read = lambda offset: v[a, pl.ds(row + offset, 1), :]
            gat[3 * a, pl.ds(j, 1), :] = read(NY) - read(-NY)
            gat[3 * a + 1, pl.ds(j, 1), :] = read(1) - read(-1)
            gat[3 * a + 2, pl.ds(j, 1), :] = read(0)
        gat[9, pl.ds(j, 1), :] = visc[pl.ds(row, 1), :]
        return carry

    lax.fori_loop(0, FLAG, gather, 0, unroll=8)

    square0, square1 = iota((FLAG, FLAG), 0), iota((FLAG, FLAG), 1)
    cell_row, owner_row = cellv[...], ownerv[...]
    cell_col, owner_col = column(cell_row), column(owner_row)
    z_col = cell_col & (NZ - 1)
    lane = iota((FLAG, NZ), 1)
    here, above, below = lane == z_col, lane == z_col + 1, lane == z_col - 1
    rank_row = jnp.sum(
        jnp.where((square0 < square1) & (owner_col == owner_row), 1, 0), axis=0, keepdims=True
    )
    rankv[...] = jnp.minimum(rank_row, 1)
    rank_copy = pltpu.make_async_copy(rankv, rank_out, out_sem.at[0])
    rank_copy.start()

    gathered = jnp.zeros((FLAG, NZ), F32)
    columns = []
    for k in range(10):
        values = gat[k]
        if k < 9 and k % 3 == 2:
            picked = jnp.where(above, values, 0.0) - jnp.where(below, values, 0.0)
        else:
            picked = jnp.where(here, values, 0.0)
        if k < 9:
            picked = picked * 0.5
        columns.append(jnp.sum(picked, axis=1, keepdims=True))
        if k < 9:
            gathered = jnp.where(lane == k, columns[k], gathered)
    position = owner_row * 2 + rank_row
    placing = (iota((SLOTS, FLAG), 0) == position).astype(F32).astype(BF16)
    hi, mid, lo = pieces(gathered, 3)
    outgoing = dot(placing, hi) + (dot(placing, mid) + dot(placing, lo))
    for s in range(owners_n):
        send1[s] = outgoing[2 * s : 2 * s + 2, :]

    @pl.when(has_up & has_down)
    def _():
        pl.semaphore_wait(barrier, owners_n + 1)

    @pl.when(jnp.logical_not(has_up & has_down))
    def _():
        pl.semaphore_wait(barrier, owners_n)

    def block_of(order, sign):
        shift = SHIFTS[order]
        return lax.rem(my_block + sign * shift + NBLOCK, NBLOCK)

    def post(order, block, send, recv, send_sem, recv_sem, own):
        if SHIFTS[order] == 0:
            own(me)
        base = block * GROUP
        turn = me - my_block * GROUP
        for k in range(1 if SHIFTS[order] == 0 else 0, GROUP):
            peer = base + lax.rem(turn + k, GROUP)
            pltpu.make_async_remote_copy(
                src_ref=send.at[peer], dst_ref=recv.at[me],
                send_sem=send_sem, recv_sem=recv_sem.at[my_block],
                device_id=peer_id(peer), device_id_type=MESH,
            ).start()

    def arrive(order, block, recv, recv_sem):
        part = recv.at[pl.ds(0, GROUP - 1 if SHIFTS[order] == 0 else GROUP)]
        pltpu.make_async_copy(part, part, recv_sem.at[block]).wait()

    def sent(send, send_sem):
        part = send.at[pl.ds(0, owners_n - 1)]
        pltpu.make_async_copy(part, part, send_sem).wait()

    def keep_row(i):
        recv1[i] = send1[i]

    def own_row(i):
        return pltpu.make_async_copy(send2.at[i], recv2.at[i], out_sem.at[1])

    for order in range(NBLOCK):
        post(order, block_of(order, -1), send1, recv1, s1_sem, r1_sem, keep_row)

    sub, lanes = iota((NY, NZ), 0), iota((NY, NZ), 1)
    face = lanes == jnp.where(micro == 0, NZ - 1, 0)
    first_lane, last_lane = lanes == 0, lanes == NZ - 1
    first_row, last_row = sub == 0, sub == NY - 1

    def rows_of(x):
        return pl.ds(x * NY, NY)

    def pack(source, names, y_pack, z_pack):
        for a, name in enumerate(names[1]):
            y_pack[0, a] = source[name, pl.ds(0, NX, stride=NY), :]
            y_pack[1, a] = source[name, pl.ds(NY - 1, NX, stride=NY), :]
        for a, name in enumerate(names[2]):
            totals = [None, None, None, None]
            for x in range(NX):
                term = jnp.where(face, source[name, rows_of(x), :], 0.0)
                if x:
                    term = pltpu.roll(term, 2 * x, 1)
                totals[x % 4] = term if totals[x % 4] is None else totals[x % 4] + term
            z_pack[a] = (totals[0] + totals[1]) + (totals[2] + totals[3])

    def exchange(x_low, x_high, y_pack, z_pack, hx, hy, hz, send_sem, recv_sem):
        def remote(i, src, dst, target):
            return pltpu.make_async_remote_copy(
                src_ref=src, dst_ref=dst, send_sem=send_sem.at[i], recv_sem=recv_sem.at[i],
                device_id=target, device_id_type=MESH,
            )

        moves = [
            (macro < n_macro - 1, macro > 0, remote(0, x_high, hx.at[0], (macro + 1, tile, micro)), hx.at[0]),
            (macro > 0, macro < n_macro - 1, remote(1, x_low, hx.at[1], (macro - 1, tile, micro)), hx.at[1]),
            (has_up, has_down, remote(2, y_pack.at[1], hy.at[0], (macro, tile + 1, micro)), hy.at[0]),
            (has_down, has_up, remote(3, y_pack.at[0], hy.at[1], (macro, tile - 1, micro)), hy.at[1]),
        ]
        beside = remote(4, z_pack, hz, (macro, tile, 1 - micro))

        def start():
            for sends, _, copy, _ in moves:
                pl.when(sends)(copy.start)
            beside.start()

        def finish():
            for _, comes, copy, landing in moves:
                pl.when(comes)(copy.wait_recv)

                @pl.when(jnp.logical_not(comes))
                def _():
                    landing[...] = jnp.zeros(landing.shape, F32)

            beside.wait_recv()

        def drain():
            for sends, _, copy, _ in moves:
                pl.when(sends)(copy.wait_send)
            beside.wait_send()

        return start, finish, drain

    def slope_x(source, name, hx, a, x):
        up = source[name, rows_of(x + 1), :] if x < NX - 1 else hx[1, a]
        down = source[name, rows_of(x - 1), :] if x > 0 else hx[0, a]
        return up - down

    def slope_y(source, name, hy, a, x):
        if x < NX - 1:
            up = source[name, pl.ds(x * NY + 1, NY), :]
        else:
            up = pltpu.roll(source[name, rows_of(x), :], NY - 1, 0)
        if x > 0:
            down = source[name, pl.ds(x * NY - 1, NY), :]
        else:
            down = pltpu.roll(source[name, rows_of(x), :], 1, 0)
        up = jnp.where(last_row, hy[1, a, pl.ds(x, 1), :], up)
        return up - jnp.where(first_row, hy[0, a, pl.ds(x, 1), :], down)

    def slope_z(source, name, hz, a, x):
        value, beside = source[name, rows_of(x), :], hz[a, rows_of(x), :]
        up = pltpu.roll(jnp.where(first_lane, beside, value), NZ - 1, 1)
        return up - pltpu.roll(jnp.where(last_lane, beside, value), 1, 1)

    def unpack(hz, layers):
        for a in range(3):
            for x in range(NX):
                layers[a, rows_of(x), :] = pltpu.roll(hz[a], NZ - 2 * x, 1) if x else hz[a]

    pack(v, ((0, 1, 2),) * 3, yp1, zp1)
    start1, finish1, drain1 = exchange(
        v.at[:, pl.ds(0, NY), :], v.at[:, pl.ds(ROWS - NY, NY), :], yp1, zp1, hx1, hy1, hz1, hs1_sem, hr1_sem
    )
    start2, finish2, drain2 = exchange(
        xp2.at[0], xp2.at[1], yp2, zp2, hx2, hy2, hz2, hs2_sem, hr2_sem
    )
    start1()

    loads[5].wait()

    def widen(t, carry):
        for a in range(3):
            nf[t, a] = nz[t, a].astype(F32) * (0.1 * SCALE)
        return carry

    lax.fori_loop(0, STEPS, widen, 0)
    loads[6].wait()
    for a in range(3):
        q[a] = q[a] * SCALE

    def chunk(c):
        return pl.ds(c * 128, 128)

    def block_work(order):
        block = block_of(order, 1)
        slots = pl.ds(pl.multiple_of(block * BLOCK, BLOCK), BLOCK)
        if order < 2:
            ready = range(1) if order == 0 else range(1, NBLOCK)
            for other in ready:
                arrive(other, block_of(other, 1), recv1, r1_sem)
            for other in ready:
                for s in range(GROUP):
                    kst[other, pl.ds(2 * s, 2), :] = recv1[block_of(other, 1) * GROUP + s]
            for other in ready:
                kappa = kst[other] * 0.01
                for k in range(9):
                    wide = jnp.broadcast_to(kappa[:, k : k + 1], (BLOCK, 128))
                    kb[other, k] = wide + 1.0 if k % 4 == 0 else wide

        def step(t, state):
            new = []
            for c in range(BEADS // 128):
                q0, q1, q2 = state[3 * c : 3 * c + 3]
                pull = pltpu.reciprocal(
                    jnp.maximum(200.0 - q0 * q0 - (q1 * q1 + q2 * q2), 20.0), approx=True
                )
                for a in range(3):
                    here_q = (q0, q1, q2)[a]
                    other = [b for b in range(3) if b != a]
                    new.append(
                        (kb[order, 4 * a] - pull) * here_q
                        + (kb[order, 3 * a + other[0]] * (q0, q1, q2)[other[0]] + kb[order, 3 * a + other[1]] * (q0, q1, q2)[other[1]])
                        + nf[t, a, slots, chunk(c)]
                    )
            return tuple(new)

        state = tuple(q[a, slots, chunk(c)] for c in range(BEADS // 128) for a in range(3))
        state = lax.fori_loop(0, STEPS, step, state, unroll=UNROLL)
        sums = [None] * 6
        for c in range(BEADS // 128):
            values = state[3 * c : 3 * c + 3]
            q0, q1, q2 = values
            pull = 1.0 / jnp.maximum(200.0 - (q0 * q0 + q1 * q1 + q2 * q2), 20.0)
            for a in range(3):
                q[a, slots, chunk(c)] = values[a] * (1.0 / SCALE)
            pulled = [pull * value for value in values]
            for k, (a, b) in enumerate(PAIRS):
                term = pulled[a] * values[b]
                sums[k] = term if sums[k] is None else sums[k] + term
        lane16 = iota((BLOCK, 128), 1)
        stresses = jnp.zeros((BLOCK, 128), F32)
        for k, (a, b) in enumerate(PAIRS):
            mean = jnp.sum(sums[k], axis=1, keepdims=True) * (30.0 / BEADS)
            stresses = jnp.where(lane16 == k, 0.25 * (mean - (1.0 if a == b else 0.0)), stresses)
        pol[...] = stresses
        for s in range(GROUP):
            send2[block * GROUP + s] = pol[pl.ds(2 * s, 2), :]
        post(order, block, send2, recv2, s2_sem, r2_sem, lambda i: own_row(i).start())

    def stress_work():
        finish1()
        unpack(hz1, layers)
        for x in range(NX):
            grad = {}
            for a in range(3):
                grad[a, 0] = slope_x(v, a, hx1, a, x)
                grad[a, 1] = slope_y(v, a, hy1, a, x)
                grad[a, 2] = slope_z(v, a, layers, a, x)
            half = visc[rows_of(x), :] * 0.5
            for k, (a, b) in enumerate(PAIRS):
                sp[k, rows_of(x), :] = half * (grad[a, b] + grad[b, a])
        for a in range(3):
            xp2[0, a] = sp[SIDE[0][a], rows_of(0), :]
            xp2[1, a] = sp[SIDE[0][a], rows_of(NX - 1), :]
        pack(sp, SIDE, yp2, zp2)
        start2()

    for order in range(NBLOCK):
        if order == STRESS_AT:
            stress_work()
        block_work(order)
    if STRESS_AT == NBLOCK:
        stress_work()

    viscous = jnp.zeros((FLAG, NZ), F32)
    for k, (a, b) in enumerate(PAIRS):
        viscous = jnp.where(lane == k, columns[9] * (columns[3 * a + b] + columns[3 * b + a]), viscous)
    vrow[...] = viscous
    vrow_copy = pltpu.make_async_copy(vrow, vrow_out, out_sem.at[2])
    vrow_copy.start()
    row_col = lax.shift_right_logical(cell_col, 7)
    six = jnp.concatenate([row_col] * 6, axis=0)
    wide0, wide1 = iota((ROWS, ROWS), 0), iota((ROWS, ROWS), 1)
    six_row = jnp.sum(jnp.where(wide0 == wide1, six, 0), axis=0, keepdims=True)
    offset = jnp.where(wide1 < 64, NY, jnp.where(wide1 < 128, 1, 0))
    plus = jnp.where(wide0 == six_row - offset, 1.0, 0.0)
    minus = jnp.where((wide0 == six_row + offset) & (wide1 < 128), 1.0, 0.0)
    amat[...] = (plus - minus).astype(BF16)
    amat_copy = pltpu.make_async_copy(amat, amat_out, out_sem.at[3])
    amat_copy.start()
    conf_copy = pltpu.make_async_copy(q, conf_out, out_sem.at[4])
    conf_copy.start()

    finish2()
    unpack(hz2, layers)
    for x in range(NX):
        for a in range(3):
            total = slope_x(sp, SIDE[0][a], hx2, a, x)
            total = total + slope_y(sp, SIDE[1][a], hy2, a, x)
            total = total + slope_z(sp, SIDE[2][a], layers, a, x)
            vel[a, rows_of(x), :] = v[a, rows_of(x), :] + 0.05 * total

    vel_copy = pltpu.make_async_copy(vel, vel_out, out_sem.at[5])
    vel_copy.start()

    drain1()
    drain2()
    sent(send1, s1_sem)
    sent(send2, s2_sem)
    for copy in (rank_copy, vrow_copy, amat_copy, conf_copy, vel_copy, own_row(me)):
        copy.wait()
    for order in range(NBLOCK):
        arrive(order, block_of(order, 1), recv2, r2_sem)


def finish(
    vel_in, conf_in, back_in, amat_in, vrow_in, rank_in, cell_in, owners_in,
    vel_out, conf_out, fs_out,
    conf, vel, back, amat, vrow, ranks, cellv, owners, prow, stress, in_sem, out_sem,
):
    loads = [
        pltpu.make_async_copy(source, target, in_sem.at[i])
        for i, (source, target) in enumerate(
            (
                (back_in, back), (rank_in, ranks), (owners_in, owners), (cell_in, cellv),
                (vrow_in, vrow), (amat_in, amat), (vel_in, vel), (conf_in, conf),
            )
        )
    ]
    for load in loads:
        load.start()
    for load in loads[:5]:
        load.wait()

    def collect(j, carry):
        prow[pl.ds(j, 1), :] = back[owners[j], pl.ds(ranks[0, j], 1), :]
        return carry

    lax.fori_loop(0, FLAG, collect, 0, unroll=True)
    lane = iota((FLAG, NZ), 1)
    z_col = column(cellv[...]) & (NZ - 1)
    here, above, below = lane == z_col, lane == z_col + 1, lane == z_col - 1
    returned = prow[...]
    flagged = vrow[...] + jnp.where(lane < 6, returned, 0.0)
    pick = (iota((8, NZ), 0) == iota((8, NZ), 1)).astype(F32).astype(BF16)
    turned = None
    for part in pieces(flagged, 3):
        term = lax.dot_general(pick, part, (((1,), (1,)), ((), ())), preferred_element_type=F32)
        turned = term if turned is None else turned + term
    stress[...] = turned[:6, :]
    stress_copy = pltpu.make_async_copy(stress, fs_out, out_sem.at[1])
    stress_copy.start()

    spread = [jnp.broadcast_to(returned[:, k : k + 1] * 0.05, (FLAG, NZ)) for k in range(6)]
    loads[7].wait()
    conf_copy = pltpu.make_async_copy(conf, conf_out, out_sem.at[0])
    conf_copy.start()
    for load in loads[5:7]:
        load.wait()
    for a in range(3):
        parts = []
        parts += pieces(jnp.where(here, spread[SIDE[0][a]], 0.0), 2)
        parts += pieces(jnp.where(here, spread[SIDE[1][a]], 0.0), 2)
        parts += pieces(
            jnp.where(below, spread[SIDE[2][a]], 0.0) - jnp.where(above, spread[SIDE[2][a]], 0.0), 2
        )
        vel[a] = vel[a] + dot(amat[...], jnp.concatenate(parts, axis=0))
        pltpu.make_async_copy(vel.at[a], vel_out.at[a], out_sem.at[2]).start()
    conf_copy.wait()
    stress_copy.wait()
    pltpu.make_async_copy(vel, vel_out, out_sem.at[2]).wait()


def shards(sizes, velocity, viscosity, flag_cell, flag_owner, conformations, increments):
    owner = flag_owner.reshape(FLAG)
    cell_row, owner_row = flag_cell.reshape(1, FLAG), flag_owner.reshape(1, FLAG)
    hbm = pl.BlockSpec(memory_space=pl.ANY)
    vmem = lambda *shape: pltpu.VMEM(shape, F32)
    shape = jax.ShapeDtypeStruct
    scratch = [
        vmem(3, ROWS, NZ), vmem(ROWS, NZ),
        pltpu.SMEM((FLAG,), I32), pltpu.VMEM((1, FLAG), I32), pltpu.VMEM((1, FLAG), I32), pltpu.VMEM((1, FLAG), I32),
        vmem(3, SLOTS, BEADS),
        pltpu.VMEM((STEPS, 3, SLOTS, BEADS), BF16), vmem(STEPS, 3, SLOTS, BEADS),
        vmem(10, FLAG, NZ), vmem(FLAG, NZ), vmem(3, ROWS, NZ),
        vmem(NBLOCK, BLOCK, 128), vmem(NBLOCK, 9, BLOCK, 128), vmem(BLOCK, 128),
        vmem(32, 2, 128), vmem(32, 2, 128), vmem(32, 2, 128),
        vmem(2, 3, NX, NZ), vmem(3, NY, NZ), vmem(2, 3, NY, NZ), vmem(2, 3, NX, NZ), vmem(3, NY, NZ),
        vmem(6, ROWS, NZ),
        vmem(2, 3, NY, NZ), vmem(2, 3, NX, NZ), vmem(3, NY, NZ),
        vmem(2, 3, NY, NZ), vmem(2, 3, NX, NZ), vmem(3, NY, NZ),
        pltpu.VMEM((ROWS, ROWS), BF16), vmem(3, ROWS, NZ),
        pltpu.SemaphoreType.DMA((7,)), pltpu.SemaphoreType.DMA((6,)),
        pltpu.SemaphoreType.DMA, pltpu.SemaphoreType.DMA((NBLOCK,)),
        pltpu.SemaphoreType.DMA, pltpu.SemaphoreType.DMA((NBLOCK,)),
        pltpu.SemaphoreType.DMA((5,)), pltpu.SemaphoreType.DMA((5,)),
        pltpu.SemaphoreType.DMA((5,)), pltpu.SemaphoreType.DMA((5,)),
    ]
    vel, conf = shape((3, ROWS, NZ), F32), shape(conformations.shape, F32)
    held = pl.pallas_call(
        functools.partial(kernel, *sizes),
        out_shape=(
            vel, conf, shape((32, 2, 128), F32), shape((ROWS, ROWS), BF16), shape((FLAG, NZ), F32),
            shape((1, FLAG), I32),
        ),
        in_specs=[hbm] * 7,
        out_specs=(hbm,) * 6,
        scratch_shapes=scratch,
        compiler_params=pltpu.CompilerParams(
            collective_id=0, has_side_effects=True, vmem_limit_bytes=56 * 2**20
        ),
    )(
        velocity.reshape(3, ROWS, NZ), viscosity.reshape(ROWS, NZ),
        flag_cell, cell_row, owner_row, conformations, increments,
    )
    vel, conf, stress = pl.pallas_call(
        finish,
        out_shape=(vel, conf, shape((6, FLAG), F32)),
        in_specs=[hbm] * 8,
        out_specs=(hbm,) * 3,
        scratch_shapes=[
            vmem(3, SLOTS, BEADS), vmem(3, ROWS, NZ), vmem(32, 2, 128), pltpu.VMEM((ROWS, ROWS), BF16), vmem(FLAG, NZ),
            pltpu.SMEM((1, FLAG), I32), pltpu.VMEM((1, FLAG), I32), pltpu.SMEM((FLAG,), I32),
            vmem(FLAG, NZ), vmem(6, FLAG),
            pltpu.SemaphoreType.DMA((8,)), pltpu.SemaphoreType.DMA((3,)),
        ],
        compiler_params=pltpu.CompilerParams(vmem_limit_bytes=56 * 2**20),
    )(*held, cell_row, owner)
    return vel.reshape(velocity.shape), conf, stress


def solution(mesh):
    sizes = (mesh.shape["macro"], mesh.shape["tile"], mesh.shape["micro"])
    in_specs = (
        P(None, "macro", "tile", "micro"),
        P("macro", "tile", "micro"),
        P(("macro", "tile", "micro")),
        P(("macro", "tile", "micro"), None),
        P(None, ("macro", "tile", "micro"), None),
        P(None, None, ("macro", "tile", "micro"), None),
    )
    out_specs = (
        P(None, "macro", "tile", "micro"),
        P(None, ("macro", "tile", "micro"), None),
        P(None, ("macro", "tile", "micro")),
    )
    return jax.shard_map(
        functools.partial(shards, sizes), mesh=mesh, in_specs=in_specs, out_specs=out_specs, check_vma=False
    )
```
